128 devices in a mesh: row: 8 (over y, x_lo), col: 8 (over x_hi, z), dir: 2 (over core).
Axes of the slice: x: 4 (x_hi: 2, x_lo: 2; x = x_hi * 2 + x_lo), y: 4, z: 4, core: 2. Of those that a mesh axis runs over, the one named last changes fastest.
Arguments:
- vis: bfloat16 [2, 8, 2048, 2048], P(None, None, 'row', 'col'), may hold values from -80 to 80, as said below
- model: bfloat16 [4, 2, 8, 2048, 2048], P('dir', None, None, 'row', 'col'), may hold values from -9 to 9, as said below
- gains: float32 [2, 4, 2, 2048], P(None, 'dir', None, 'col'), may hold values from -4 to 4
- channel_interval_index: int32 [4, 8], replicated, may hold values from 0 to 1
- antenna_usable_mask: int32 [8, 2048], replicated, may hold values 0 or 1
Outputs:
- gains_new: float32 [2, 4, 2, 2048], P(None, 'dir', None, 'col')
- residual: float32 [2, 8, 2048, 2048], P(None, 'dir', 'row', 'col')
The draws below stay inside these ranges and needn't reach their ends.
Inputs may be any that keep to these rules, and one draw needn't show every extreme that they name: For every channel vis is Hermitian in its last two dimensions: vis[0, c, p, q] = vis[0, c, q, p] and vis[1, c, p, q] = -vis[1, c, q, p]. For every direction and channel model is Hermitian in its last two dimensions: model[d, 0, c, p, q] = model[d, 0, c, q, p] and model[d, 1, c, p, q] = -model[d, 1, c, q, p].
All inputs are finite; a program needn't handle non-finite values.
Results may differ from the reference program's by a relative error of at most 0.0006.
Values may be sent and summed in bfloat16 or wider, within the bound.
A program may use at most 64 MiB of HBM per device.

```python
import math
import jax
import jax.numpy as jnp
from jax import lax

ANTENNA_COUNT = 2048
CHANNEL_COUNT = 8
NDIR = 4
NG = 2
ITERS = 2


def truth(key):
    base = jax.random.fold_in(key, 100)
    key_amp, key_phase, key_bright = jax.random.split(base, 3)
    amplitude = jnp.exp(jax.random.uniform(key_amp, (NDIR, ANTENNA_COUNT), jnp.float32, math.log(0.6), math.log(1.5)))
    phase = jax.random.uniform(key_phase, (NDIR, ANTENNA_COUNT), jnp.float32, -math.pi, math.pi)
    bright = jnp.exp(jax.random.uniform(key_bright, (NDIR,), jnp.float32, math.log(0.3), math.log(1.2)))
    return (amplitude * jnp.cos(phase), amplitude * jnp.sin(phase), bright)


def model_raw(key):
    base = jax.random.fold_in(key, 7)
    key_real, key_imag = jax.random.split(base)
    first = jnp.clip(jax.random.normal(key_real, (NDIR, CHANNEL_COUNT, ANTENNA_COUNT, ANTENNA_COUNT), jnp.float32), -5.0, 5.0)
    second = jnp.clip(jax.random.normal(key_imag, (NDIR, CHANNEL_COUNT, ANTENNA_COUNT, ANTENNA_COUNT), jnp.float32), -5.0, 5.0)
    bright = truth(key)[2][:, None, None, None]
    model_re = (first + jnp.swapaxes(first, -1, -2)) * 0.5 ** 0.5 * bright
    model_im = (second - jnp.swapaxes(second, -1, -2)) * 0.5 ** 0.5 * bright
    return (model_re, model_im)


def draw_model(key, part):
    model_re, model_im = model_raw(key)
    return jnp.stack([model_re, model_im], axis=1).astype(jnp.bfloat16)


def draw_vis(key, part):
    model_re, model_im = model_raw(key)
    true_re, true_im = (truth(key)[0], truth(key)[1])
    rows_re = true_re[:, None, :, None]
    rows_im = true_im[:, None, :, None]
    cols_re = true_re[:, None, None, :]
    cols_im = true_im[:, None, None, :]
    left_re = rows_re * model_re - rows_im * model_im
    left_im = rows_re * model_im + rows_im * model_re
    sky_re = jnp.sum(left_re * cols_re + left_im * cols_im, axis=0)
    sky_im = jnp.sum(left_im * cols_re - left_re * cols_im, axis=0)
    key = jax.random.fold_in(key, 2)
    key_real, key_imag = jax.random.split(key)
    first = 0.3 * jnp.clip(jax.random.normal(key_real, (CHANNEL_COUNT, ANTENNA_COUNT, ANTENNA_COUNT), jnp.float32), -5.0, 5.0)
    second = 0.3 * jnp.clip(jax.random.normal(key_imag, (CHANNEL_COUNT, ANTENNA_COUNT, ANTENNA_COUNT), jnp.float32), -5.0, 5.0)
    total_re = sky_re + first
    total_im = sky_im + second
    visibility_real = (total_re + jnp.swapaxes(total_re, -1, -2)) * 0.5
    vis_im = (total_im - jnp.swapaxes(total_im, -1, -2)) * 0.5
    return jnp.stack([visibility_real, vis_im]).astype(jnp.bfloat16)


def draw_gains(key, part):
    true_re, true_im = (truth(key)[0], truth(key)[1])
    key = jax.random.fold_in(key, 3)
    noise = jnp.clip(0.35 * jax.random.normal(key, (2, NDIR, NG, ANTENNA_COUNT), jnp.float32), -0.6, 0.6)
    base_re = true_re[:, None, :]
    base_im = true_im[:, None, :]
    gain_re = base_re * (1.0 + noise[0]) - base_im * noise[1]
    gain_im = base_re * noise[1] + base_im * (1.0 + noise[0])
    return jnp.stack([gain_re, gain_im])


def plant(values, stream_key, low, high):
    longest = values.shape.index(max(values.shape))
    spots = []
    for shift in (0, 1):
        where = [jax.random.randint(jax.random.fold_in(stream_key, axis), (), 0, length) for axis, length in enumerate(values.shape)]
        where[longest] = (where[longest] + shift) % values.shape[longest]
        spots.append(tuple(where))
    return values.at[spots[0]].set(low).at[spots[1]].set(high)


def setup_inputs(seed: int = 0) -> dict:
    seeds = jax.random.split(jax.random.key(seed), 6)
    return {
        "vis": draw_vis(jax.random.fold_in(seeds[5], 71), 0),
        "model": draw_model(jax.random.fold_in(seeds[5], 71), 0),
        "gains": draw_gains(jax.random.fold_in(seeds[5], 71), 0),
        "channel_interval_index": plant(jax.random.randint(seeds[3], (NDIR, CHANNEL_COUNT), 0, NG), jax.random.fold_in(seeds[3], 1), 0, NG - 1).astype(jnp.int32),
        "antenna_usable_mask": plant((jax.random.randint(seeds[4], (CHANNEL_COUNT, ANTENNA_COUNT), 0, 10) < 9).astype(jnp.int32), jax.random.fold_in(seeds[4], 1), 0, 1),
    }


def expand(gain_set, onehot):
    return jnp.einsum("dck,xdkp->xdcp", onehot, gain_set, precision=lax.Precision.HIGHEST)


def collect(values, onehot):
    return jnp.einsum("dck,xdcp->xdkp", onehot, values, precision=lax.Precision.HIGHEST)


def collect_den(values, onehot):
    return jnp.einsum("dck,dcp->dkp", onehot, values, precision=lax.Precision.HIGHEST)


def predict(model_re, model_im, rows_re, rows_im, cols_re, cols_im):
    left_re = rows_re[:, :, None] * model_re - rows_im[:, :, None] * model_im
    left_im = rows_re[:, :, None] * model_im + rows_im[:, :, None] * model_re
    pred_re = left_re * cols_re[:, None, :] + left_im * cols_im[:, None, :]
    pred_im = left_im * cols_re[:, None, :] - left_re * cols_im[:, None, :]
    return pred_re, pred_im


def refresh(current, numer, denom):
    fresh = (numer + current) / (denom[None] + 1.0)
    return 0.5 * (fresh + current)


def reference(vis, model, gains, channel_interval_index, antenna_usable_mask):
    onehot = (channel_interval_index[:, :, None] == jnp.arange(NG, dtype=jnp.int32)[None, None, :]).astype(jnp.float32)
    flag_mask = antenna_usable_mask.astype(jnp.float32)
    index = jnp.arange(ANTENNA_COUNT, dtype=jnp.int32)
    offdiag = (index[:, None] != index[None, :]).astype(jnp.float32)
    weight = flag_mask[:, :, None] * flag_mask[:, None, :] * offdiag[None]
    visibility_real = vis[0].astype(jnp.float32)
    vis_im = vis[1].astype(jnp.float32)

    def one_pred(full, which):
        return predict(model[which, 0].astype(jnp.float32), model[which, 1].astype(jnp.float32),
                       full[0, which], full[1, which], full[0, which], full[1, which])

    def total_pred(full):
        total_re = jnp.zeros_like(visibility_real)
        total_im = jnp.zeros_like(vis_im)
        for which in range(NDIR):
            pred_re, pred_im = one_pred(full, which)
            total_re = total_re + pred_re
            total_im = total_im + pred_im
        return total_re, total_im

    current = gains
    for sweep in range(ITERS):
        full = expand(current, onehot)
        total_re, total_im = total_pred(full)
        res_re = visibility_real - total_re
        res_im = vis_im - total_im
        num_re, num_im, den_all = [], [], []
        for which in range(NDIR):
            pred_re, pred_im = one_pred(full, which)
            data_re = res_re + pred_re
            data_im = res_im + pred_im
            model_re = model[which, 0].astype(jnp.float32)
            model_im = model[which, 1].astype(jnp.float32)
            cols_re = full[0, which][:, None, :]
            cols_im = full[1, which][:, None, :]
            pair_re = model_re * cols_re + model_im * cols_im
            pair_im = model_im * cols_re - model_re * cols_im
            num_re.append(jnp.sum(weight * (data_re * pair_re + data_im * pair_im), axis=2))
            num_im.append(jnp.sum(weight * (data_im * pair_re - data_re * pair_im), axis=2))
            den_all.append(jnp.sum(weight * (pair_re * pair_re + pair_im * pair_im), axis=2))
        numer = collect(jnp.stack([jnp.stack(num_re), jnp.stack(num_im)]), onehot)
        denom = collect_den(jnp.stack(den_all), onehot)
        current = refresh(current, numer, denom)
    total_re, total_im = total_pred(expand(current, onehot))
    residual = jnp.stack([visibility_real - total_re, vis_im - total_im])
    return current, residual
```

```python
import functools

import jax
import jax.numpy as jnp
from jax import lax
from jax.experimental import pallas as pl
from jax.experimental.pallas import tpu as pltpu
from jax.sharding import PartitionSpec as P

ITERS = 2
MESH = pl.DeviceIdType.MESH
F32, BF16 = jnp.float32, jnp.bfloat16
TILE = 16


def rows_like(shape):
    return lax.broadcasted_iota(jnp.int32, shape, 0)


def turned(g):
    count = g.shape[0] // 8
    out = []
    for k in range(count):
        out += [-g[8 * k + 4 : 8 * k + 8], g[8 * k : 8 * k + 4]]
    return jnp.concatenate(out, axis=0)


def halves(x):
    high = x.astype(BF16)
    return high, (x - high.astype(F32)).astype(BF16)


def outer_products(a_ref, g_rows, g_cols):
    width = g_cols.shape[1]
    right = jnp.concatenate([g_cols, turned(g_cols)], axis=1)
    right_hi, right_lo = halves(right)
    right_all = jnp.concatenate([right_hi, right_lo, right_hi], axis=0)
    left_hi, left_lo = halves(g_rows)
    row = rows_like((48, g_rows.shape[1]))
    left_all = jnp.concatenate([left_hi, left_hi, left_lo], axis=0).astype(F32)
    for k in range(2):
        for d in range(4):
            at = row % 16
            keep = (at == 8 * k + d) | (at == 8 * k + 4 + d)
            left = jnp.where(keep, left_all, 0.0).astype(BF16)
            a_ref[k * 4 + d] = lax.dot_general(
                left, right_all, (((0,), (0,)), ((), ())), preferred_element_type=F32
            )


def channel_rows(g, picks):
    at = rows_like((8, g.shape[1])) % 4
    second = jnp.zeros(at.shape, jnp.int32)
    for d in range(4):
        second = jnp.where(at == d, picks[d], second)
    return jnp.where(second == 1, g[8:16], g[0:8]), second


def kernel(
    n_row, n_col,
    vis, model, gains, mask, idx,
    gains_out, res_out,
    m_v, v_v, mf_v, vf_v, d_v, a_v, a2_v, t_v, off_v, fr_v, fc_v, fri_v, fci_v, out_v,
    gin_c, gin_r, g_r, g_c, g_r2, colb, rowb,
    loc_sem, out_sem, mod_s, mod_r, gs_s, gs_r, gr_s, gr_r, col_s, col_r, row_s, row_r, fin_s, fin_r,
):
    r, c, e = lax.axis_index("row"), lax.axis_index("col"), lax.axis_index("dir")
    other = 1 - e
    sib = (r, c, other)
    half = model.shape[3] // 2
    chans = model.shape[2]
    fin = chans // 2

    def row_peer(k, x):
        return lax.rem(r + k, n_row), c, lax.rem(e + x, 2)

    def col_peer(k, x):
        return r, lax.rem(c + k, n_col), lax.rem(e + x, 2)

    row_list = [(k, x) for k in range(n_row) for x in range(2) if (k, x) != (0, 0)]
    col_list = [(k, x) for k in range(1, n_col) for x in range(2)]

    barrier = pltpu.get_barrier_semaphore()
    for k, x in col_list:
        pl.semaphore_signal(barrier, inc=1, device_id=col_peer(k, x), device_id_type=MESH)
    for k, x in row_list:
        pl.semaphore_signal(barrier, inc=1, device_id=row_peer(k, x), device_id_type=MESH)

    mine = pl.ds(pl.multiple_of(e * half, half), half)
    theirs = pl.ds(pl.multiple_of(other * half, half), half)
    my_ch = pl.ds(e * fin, fin)
    their_ch = pl.ds(other * fin, fin)
    block_r = pl.ds(pl.multiple_of(r * 2 * half + e * half, half), half)
    block_c = pl.ds(pl.multiple_of(c * 2 * half, 2 * half), 2 * half)
    local = [
        (gains, gin_c.at[e]),
        (mask.at[:, block_r], fri_v),
        (mask.at[:, block_c], fci_v),
        (vis.at[:, :, mine, :], v_v),
        (vis.at[:, my_ch, theirs, :], vf_v),
        (model.at[:, :, :, mine, :], m_v.at[pl.ds(2 * e, 2)]),
        (model.at[:, :, my_ch, theirs, :], mf_v.at[pl.ds(2 * e, 2)]),
    ]
    local = [pltpu.make_async_copy(s, d, loc_sem.at[i]) for i, (s, d) in enumerate(local)]
    for cp in local:
        cp.start()

    def remote(src, dst, send, recv, device):
        return pltpu.make_async_remote_copy(
            src_ref=src, dst_ref=dst, send_sem=send, recv_sem=recv,
            device_id=device, device_id_type=MESH,
        )

    local[0].wait()
    pl.semaphore_wait(barrier, len(col_list) + len(row_list))

    gains_sib = remote(gin_c.at[e], gin_c.at[e], gs_s, gs_r, sib)
    diag = r == c

    @pl.when(diag)
    def _():
        for i, (k, x) in enumerate(col_list):
            remote(gin_c.at[e], gin_r.at[e], gr_s.at[i], gr_r.at[e], col_peer(k, x)).start()

    gains_sib.start()
    model_a = remote(
        model.at[:, :, :, theirs, :], m_v.at[pl.ds(2 * e, 2)], mod_s.at[0], mod_r.at[0], sib
    )
    model_b = remote(
        model.at[:, :, their_ch, mine, :], mf_v.at[pl.ds(2 * e, 2)], mod_s.at[1], mod_r.at[1], sib
    )
    model_a.start()
    model_b.start()

    for cp in local[1:]:
        cp.wait()
    fr_v[...] = fri_v[...].astype(F32)
    fc_v[...] = fci_v[...].astype(F32)
    p_at = r * 2 * half + e * half + rows_like(off_v.shape)
    q_at = c * 2 * half + lax.broadcasted_iota(jnp.int32, off_v.shape, 1)
    off_v[...] = jnp.where(p_at == q_at, 0.0, 1.0).astype(BF16)

    gains_sib.wait_recv()
    for s in range(2):
        for x in range(2):
            for l in range(2):
                for k in range(2):
                    at = k * 8 + x * 4 + s * 2 + l
                    g_c[at : at + 1, :] = gin_c[s, x, l, k : k + 1, :]

    model_a.wait_recv()

    def squares(ch, _):
        for d in range(4):
            for t in range(half // TILE):
                rows = slice(t * TILE, (t + 1) * TILE)
                re = m_v[d, 0, ch, rows, :].astype(F32)
                im = m_v[d, 1, ch, rows, :].astype(F32)
                sq = (re * re + im * im).astype(BF16) * off_v[rows, :]
                at = (d % 2) * half + t * TILE
                d_v[ch, d // 2, at : at + TILE, :] = sq
        return 0

    lax.fori_loop(0, chans, squares, 0)

    @pl.when(diag)
    def _():
        gin_r[...] = gin_c[...]

    @pl.when(jnp.logical_not(diag))
    def _():
        for s in range(2):
            remote(gin_c.at[s], gin_r.at[s], gr_s.at[0], gr_r.at[s], sib).wait_recv()

    lanes = pl.ds(pl.multiple_of(e * half, half), half)
    for s in range(2):
        for x in range(2):
            for l in range(2):
                for k in range(2):
                    at = k * 8 + x * 4 + s * 2 + l
                    g_r[at : at + 1, :] = gin_r[s, x, l, k : k + 1, lanes]

    def residual_tile(a, mod, vi, ch, picks, rows):
        re = vi[0, ch, rows, :].astype(F32)
        im = vi[1, ch, rows, :].astype(F32)
        width = re.shape[1]
        for d in range(4):
            at = picks[d] * 4 + d
            a_re = a[at, rows, 0:width]
            a_im = a[at, rows, width : 2 * width]
            m_re = mod[d, 0, ch, rows, :].astype(F32)
            m_im = mod[d, 1, ch, rows, :].astype(F32)
            re = re - a_re * m_re + a_im * m_im
            im = im - a_re * m_im - a_im * m_re
        return re, im

    def sweep(step):
        gr, gc = g_r[...], g_c[...]
        outer_products(a_v, gr, gc)
        zeros_c = jnp.zeros((24, gc.shape[1]), F32)
        zeros_r = jnp.zeros((24, gr.shape[1]), F32)

        def channel(ch, carry):
            col, row = carry
            picks = [idx[d, ch] for d in range(4)]
            for t in range(half // TILE):
                rows = slice(t * TILE, (t + 1) * TILE)
                re, im = residual_tile(a_v, m_v, v_v, ch, picks, rows)
                re = re.astype(BF16) * off_v[rows, :]
                im = im.astype(BF16) * off_v[rows, :]
                for d in range(4):
                    m_re = m_v[d, 0, ch, rows, :]
                    m_im = m_v[d, 1, ch, rows, :]
                    t_v[d, t * TILE : (t + 1) * TILE, :] = re * m_re + im * m_im
                    at = half + t * TILE
                    t_v[d, at : at + TILE, :] = re * m_im - im * m_re
            f_r = fr_v[pl.ds(ch, 1), :]
            f_c = fc_v[pl.ds(ch, 1), :]
            x_r, second_r = channel_rows(gr, picks)
            x_c, second_c = channel_rows(gc, picks)
            x_r = x_r * f_r
            x_c = x_c * f_c
            x_col = jnp.concatenate([x_r, turned(x_r)], axis=1).astype(BF16)
            x_row = x_c.astype(BF16)
            at_c = rows_like(x_c.shape) % 4
            o_col = jnp.zeros(x_c.shape, F32)
            o_row = jnp.zeros(x_c.shape, F32)
            for d in range(4):
                got = jnp.dot(x_col, t_v[d], preferred_element_type=F32)
                o_col = jnp.where(at_c == d, got, o_col)
                got = lax.dot_general(
                    x_row, t_v[d], (((1,), (1,)), ((), ())), preferred_element_type=F32
                )
                o_row = jnp.where(at_c == d, got, o_row)
            back = -turned(o_row[:, half:])
            o_row = o_row[:, :half] + back
            s_r = x_r[0:4] * x_r[0:4] + x_r[4:8] * x_r[4:8]
            s_c = x_c[0:4] * x_c[0:4] + x_c[4:8] * x_c[4:8]
            at_4 = rows_like(s_r.shape)
            at_4c = rows_like(s_c.shape)
            den_c = jnp.zeros(s_c.shape, F32)
            den_r = jnp.zeros(s_r.shape, F32)
            for pair in range(2):
                left = jnp.concatenate(
                    [jnp.where(at_4 == 2 * pair + i, s_r, 0.0) for i in range(2)], axis=1
                ).astype(BF16)
                den_c += jnp.dot(left, d_v[ch, pair], preferred_element_type=F32)
                got = lax.dot_general(
                    s_c.astype(BF16), d_v[ch, pair], (((1,), (1,)), ((), ())),
                    preferred_element_type=F32,
                )
                for i in range(2):
                    den_r = jnp.where(at_4 == 2 * pair + i, got[:, i * half : (i + 1) * half], den_r)
            col_new = jnp.concatenate([o_col, den_c], axis=0) * f_c
            row_new = jnp.concatenate([o_row, den_r], axis=0) * f_r
            pick_c = jnp.concatenate([second_c, second_c[0:4]], axis=0) == 1
            pick_r = jnp.concatenate([second_r, second_r[0:4]], axis=0) == 1
            col = col + jnp.concatenate(
                [jnp.where(pick_c, 0.0, col_new), jnp.where(pick_c, col_new, 0.0)], axis=0
            )
            row = row + jnp.concatenate(
                [jnp.where(pick_r, 0.0, row_new), jnp.where(pick_r, row_new, 0.0)], axis=0
            )
            return col, row

        col, row = lax.fori_loop(0, chans, channel, (zeros_c, zeros_r))
        colb[step, r * 2 + e] = col
        rowb[step, c] = row
        col_copies, row_copies = [], []
        own = r * 2 + e
        for i in range(1, n_col):
            cp = remote(
                rowb.at[step, c], rowb.at[step, c], row_s.at[step, i], row_r.at[step, c],
                col_peer(i, 0),
            )
            cp.start()
            row_copies.append(cp)
        for i, (k, x) in enumerate(row_list):
            cp = remote(
                colb.at[step, own], colb.at[step, own], col_s.at[step, i], col_r.at[step, own],
                row_peer(k, x),
            )
            cp.start()
            col_copies.append(cp)
        for i in range(1, n_col):
            src = lax.rem(c + i, n_col)
            remote(
                rowb.at[step, src], rowb.at[step, src], row_s.at[step, i], row_r.at[step, src],
                col_peer(i, 0),
            ).wait_recv()
        for i, (k, x) in enumerate(row_list):
            src = lax.rem(r + k, n_row) * 2 + lax.rem(e + x, 2)
            remote(
                colb.at[step, src], colb.at[step, src], col_s.at[step, i], col_r.at[step, src],
                row_peer(k, x),
            ).wait_recv()

        def refresh(g, total):
            out = []
            for k in range(2):
                den = total[12 * k + 8 : 12 * k + 12] + 1.0
                den = jnp.concatenate([den, den], axis=0)
                out.append(g[8 * k : 8 * k + 8] + 0.5 * total[12 * k : 12 * k + 8] / den)
            return jnp.concatenate(out, axis=0)

        total = rowb[step, 0]
        for i in range(1, n_col):
            total = total + rowb[step, i]
        g_r[...] = refresh(gr, total)
        total = colb[step, 0]
        for i in range(1, 2 * n_row):
            total = total + colb[step, i]
        g_c[...] = refresh(gc, total)
        return col_copies + row_copies

    copies = []
    for step in range(ITERS):
        copies += sweep(step)

    g_r2[e] = g_r[...]
    rows_sib = remote(g_r2.at[e], g_r2.at[e], fin_s, fin_r, sib)
    rows_sib.start()

    for x in range(2):
        for l in range(2):
            for k in range(2):
                at = k * 8 + x * 4 + l
                gains_out[x, l, k : k + 1, :] = jnp.where(
                    e == 0, g_c[at : at + 1, :], g_c[at + 2 : at + 3, :]
                )

    def finish(a, mod, vi, where, base, which):
        def channel(ch, _):
            picks = [idx[d, e * fin + ch] for d in range(4)]
            for t in range(half // TILE):
                rows = slice(t * TILE, (t + 1) * TILE)
                re, im = residual_tile(a, mod, vi, base + ch, picks, rows)
                out_v[which, 0, ch, rows, :] = re
                out_v[which, 1, ch, rows, :] = im
            pltpu.make_async_copy(
                out_v.at[which, :, ch], res_out.at[:, ch, where, :], out_sem.at[which, ch]
            ).start()
            return 0

        lax.fori_loop(0, fin, channel, 0)

    outer_products(a_v, g_r[...], g_c[...])
    finish(a_v, m_v, v_v, mine, e * fin, 0)
    rows_back = remote(g_r2.at[other], g_r2.at[other], fin_s, fin_r, sib)
    rows_back.wait_recv()
    outer_products(a2_v, g_r2[other], g_c[...])
    model_b.wait_recv()
    finish(a2_v, mf_v, vf_v, theirs, 0, 1)

    model_a.wait_send()
    model_b.wait_send()
    gains_sib.wait_send()

    @pl.when(diag)
    def _():
        for i, (k, x) in enumerate(col_list):
            remote(gin_c.at[e], gin_r.at[e], gr_s.at[i], gr_r.at[e], col_peer(k, x)).wait_send()

    for cp in copies:
        cp.wait_send()
    rows_sib.wait_send()
    for which, where in enumerate((mine, theirs)):
        for ch in range(fin):
            pltpu.make_async_copy(
                out_v.at[which, :, ch], res_out.at[:, ch, where, :], out_sem.at[which, ch]
            ).wait()


def body(n_row, n_col, vis, model, gains, channel_interval_index, antenna_usable_mask):
    dirs, _, chans, rows, cols = model.shape
    half = rows // 2
    fin = chans // 2
    n_dir = 2 * dirs
    any_space = pl.BlockSpec(memory_space=pl.ANY)
    dma = pltpu.SemaphoreType.DMA
    return pl.pallas_call(
        functools.partial(kernel, n_row, n_col),
        out_shape=(
            jax.ShapeDtypeStruct(gains.shape, F32),
            jax.ShapeDtypeStruct((2, fin, rows, cols), F32),
        ),
        in_specs=[any_space] * 4 + [pl.BlockSpec(memory_space=pltpu.SMEM)],
        out_specs=(pl.BlockSpec(memory_space=pltpu.VMEM), any_space),
        scratch_shapes=[
            pltpu.VMEM((n_dir, 2, chans, half, cols), BF16),
            pltpu.VMEM((2, chans, half, cols), BF16),
            pltpu.VMEM((n_dir, 2, fin, half, cols), BF16),
            pltpu.VMEM((2, fin, half, cols), BF16),
            pltpu.VMEM((chans, 2, 2 * half, cols), BF16),
            pltpu.VMEM((8, half, 2 * cols), F32),
            pltpu.VMEM((8, half, 2 * cols), F32),
            pltpu.VMEM((n_dir, 2 * half, cols), BF16),
            pltpu.VMEM((half, cols), BF16),
            pltpu.VMEM((chans, half), F32),
            pltpu.VMEM((chans, cols), F32),
            pltpu.VMEM((chans, half), jnp.int32),
            pltpu.VMEM((chans, cols), jnp.int32),
            pltpu.VMEM((2, 2, fin, half, cols), F32),
            pltpu.VMEM((2,) + gains.shape, F32),
            pltpu.VMEM((2,) + gains.shape, F32),
            pltpu.VMEM((16, half), F32),
            pltpu.VMEM((16, cols), F32),
            pltpu.VMEM((2, 16, half), F32),
            pltpu.VMEM((ITERS, 2 * n_row, 24, cols), F32),
            pltpu.VMEM((ITERS, n_col, 24, half), F32),
            dma((7,)),
            dma((2, fin)),
            dma((2,)),
            dma((2,)),
            dma,
            dma,
            dma((2 * n_col,)),
            dma((2,)),
            dma((ITERS, 2 * n_row)),
            dma((ITERS, 2 * n_row)),
            dma((ITERS, n_col)),
            dma((ITERS, n_col)),
            dma,
            dma,
        ],
        compiler_params=pltpu.CompilerParams(
            collective_id=0, has_side_effects=True, vmem_limit_bytes=48 * 2**20
        ),
    )(vis, model, gains, antenna_usable_mask, channel_interval_index)


def solution(mesh):
    placed = (
        P(None, None, "row", "col"),
        P("dir", None, None, "row", "col"),
        P(None, "dir", None, "col"),
        P(),
        P(),
    )
    return jax.shard_map(
        functools.partial(body, mesh.shape["row"], mesh.shape["col"]),
        mesh=mesh,
        in_specs=placed,
        out_specs=(P(None, "dir", None, "col"), P(None, "dir", "row", "col")),
        check_vma=False,
    )
```

```python
import functools

import jax
import jax.numpy as jnp
from jax import lax
from jax.experimental import pallas as pl
from jax.experimental.pallas import tpu as pltpu
from jax.sharding import PartitionSpec as P

ITERS = 2
MESH = pl.DeviceIdType.MESH
F32, BF16 = jnp.float32, jnp.bfloat16
TILE = 16


def rows_like(shape):
    return lax.broadcasted_iota(jnp.int32, shape, 0)


def turned(g):
    count = g.shape[0] // 8
    out = []
    for k in range(count):
        out += [-g[8 * k + 4 : 8 * k + 8], g[8 * k : 8 * k + 4]]
    return jnp.concatenate(out, axis=0)


def halves(x):
    high = x.astype(BF16)
    return high, (x - high.astype(F32)).astype(BF16)


def outer_products(a_ref, g_rows, g_cols):
    width = g_cols.shape[1]
    right = jnp.concatenate([g_cols, turned(g_cols)], axis=1)
    right_hi, right_lo = halves(right)
    right_all = jnp.concatenate([right_hi, right_lo, right_hi], axis=0)
    left_hi, left_lo = halves(g_rows)
    row = rows_like((48, g_rows.shape[1]))
    left_all = jnp.concatenate([left_hi, left_hi, left_lo], axis=0).astype(F32)
    for k in range(2):
        for d in range(4):
            at = row % 16
            keep = (at == 8 * k + d) | (at == 8 * k + 4 + d)
            left = jnp.where(keep, left_all, 0.0).astype(BF16)
            a_ref[k * 4 + d] = lax.dot_general(
                left, right_all, (((0,), (0,)), ((), ())), preferred_element_type=F32
            )


def residual_tile(a, mod, vi, ch, picks, rows):
    re = vi[0, ch, rows, :].astype(F32)
    im = vi[1, ch, rows, :].astype(F32)
    width = re.shape[1]
    for d in range(4):
        at = picks[d] * 4 + d
        a_re = a[at, rows, 0:width]
        a_im = a[at, rows, width : 2 * width]
        m_re = mod[d, 0, ch, rows, :].astype(F32)
        m_im = mod[d, 1, ch, rows, :].astype(F32)
        re = re - a_re * m_re + a_im * m_im
        im = im - a_re * m_im - a_im * m_re
    return re, im


def kernel(
    n_row, n_col,
    vis, model, gains, mask, index,
    m_v, v_v, mf_v, vf_v, g_r2, g_c, idx,
    w_v, d_v, a_v, t_v, fri_v, fci_v, prev, last,
    gin_c, gin_r, g_r, colb, rowb, colt,
    loc_sem, mod_s, mod_r, gs_s, gs_r, gr_s, gr_r,
    col_s, col_r, row_s, row_r, ct_s, ct_r, fin_s, fin_r,
):
    r, c, e = lax.axis_index("row"), lax.axis_index("col"), lax.axis_index("dir")
    other = 1 - e
    sib = (r, c, other)
    half = model.shape[3] // 2
    chans = model.shape[2]
    fin = chans // 2
    quad = n_col // 2

    def row_peer(k):
        return lax.rem(r + k, n_row), c, e

    def col_peer(k):
        return r, lax.rem(c + k, n_col), e

    row_list = sorted(range(1, n_row), key=lambda k: (k % 2 == 0, abs(k - n_row // 2)))
    col_list = sorted(range(1, n_col), key=lambda k: abs(k - n_col // 2))

    flip_r = r + 1 - 2 * lax.rem(r, 2)
    flip_c = c + 1 - 2 * lax.rem(c, 2)
    near = r == c
    cross = r == flip_c
    same = lax.div(r, quad) == lax.div(c, quad)
    source_row = jnp.where(same, r, flip_r)
    near_to = [
        (r, lax.div(c, quad) * quad + lax.rem(c + k, quad), x)
        for k in range(1, quad) for x in range(2)
    ]
    cross_to = [
        (c, (1 - lax.div(c, quad)) * quad + k, x) for k in range(quad) for x in range(2)
    ]

    barrier = pltpu.get_barrier_semaphore()

    @pl.when(jnp.logical_not(near))
    def _():
        for x in range(2):
            pl.semaphore_signal(
                barrier, inc=1, device_id=(source_row, r, x), device_id_type=MESH
            )

    for k in col_list:
        pl.semaphore_signal(barrier, inc=1, device_id=col_peer(k), device_id_type=MESH)
    for k in row_list:
        pl.semaphore_signal(barrier, inc=1, device_id=row_peer(k), device_id_type=MESH)
    pl.semaphore_signal(barrier, inc=1, device_id=sib, device_id_type=MESH)

    mine = pl.ds(pl.multiple_of(e * half, half), half)
    theirs = pl.ds(pl.multiple_of(other * half, half), half)
    my_ch = pl.ds(e * fin, fin)
    their_ch = pl.ds(other * fin, fin)
    block_r = pl.ds(pl.multiple_of(r * 2 * half + e * half, half), half)
    block_c = pl.ds(pl.multiple_of(c * 2 * half, 2 * half), 2 * half)
    own_dirs = pl.ds(2 * e, 2)
    local = [
        (gains, gin_c.at[e]),
        (index, idx),
        (mask.at[:, block_r], fri_v),
        (mask.at[:, block_c], fci_v),
        (model.at[:, :, :, mine, :], m_v.at[own_dirs]),
        (vis.at[:, :, mine, :], v_v),
        (vis.at[:, my_ch, theirs, :], vf_v),
        (model.at[:, :, my_ch, theirs, :], mf_v.at[own_dirs]),
    ]
    local = [pltpu.make_async_copy(s, d, loc_sem.at[i]) for i, (s, d) in enumerate(local)]
    for cp in local:
        cp.start()

    def remote(src, dst, send, recv, device):
        return pltpu.make_async_remote_copy(
            src_ref=src, dst_ref=dst, send_sem=send, recv_sem=recv,
            device_id=device, device_id_type=MESH,
        )

    local[0].wait()
    n_near, n_cross = len(near_to), len(cross_to)
    pl.semaphore_wait(
        barrier,
        len(col_list) + len(row_list) + 1
        + jnp.where(near, n_near, 0) + jnp.where(cross, n_cross, 0),
    )

    def gains_to(devices):
        return [
            remote(gin_c.at[e], gin_r.at[e], gr_s.at[i], gr_r.at[e], to)
            for i, to in enumerate(devices)
        ]

    @pl.when(near)
    def _():
        for cp in gains_to(near_to):
            cp.start()

    @pl.when(cross)
    def _():
        for cp in gains_to(cross_to):
            cp.start()

    gains_sib = remote(gin_c.at[e], gin_c.at[e], gs_s, gs_r, sib)
    gains_sib.start()
    model_a = [
        remote(
            model.at[l, :, :, theirs, :], m_v.at[2 * e + l], mod_s.at[l], mod_r.at[l], sib
        )
        for l in range(2)
    ]
    model_b = remote(
        model.at[:, :, their_ch, mine, :], mf_v.at[own_dirs], mod_s.at[2], mod_r.at[2], sib
    )
    for cp in model_a:
        cp.start()
    model_b.start()

    for cp in local[1:4]:
        cp.wait()
    for d in range(4):
        ends = [jnp.int32(chans), jnp.int32(chans)]
        for ch in range(chans):
            second = idx[d, ch] == 1
            prev[d, ch] = jnp.where(second, ends[1], ends[0])
            ends = [jnp.where(second, ends[0], ch), jnp.where(second, ch, ends[1])]
        for k in range(2):
            last[k, d] = ends[k]
    t_v[chans] = jnp.zeros(t_v.shape[1:], BF16)
    shape = (half, 2 * half)
    p_at = r * 2 * half + e * half + rows_like(shape)
    q_at = c * 2 * half + lax.broadcasted_iota(jnp.int32, shape, 1)
    apart = p_at != q_at
    f_r = fri_v[...].astype(F32)
    f_c = fci_v[...].astype(F32).astype(BF16)
    for ch in range(chans):
        one = jnp.where(rows_like(f_r.shape) == ch, f_r, 0.0).astype(BF16)
        both = lax.dot_general(
            one, f_c, (((0,), (0,)), ((), ())), preferred_element_type=F32
        )
        w_v[ch] = jnp.where(apart, both, 0.0).astype(BF16)

    def squares(core, l):
        d = 2 * core + l

        def tile(t, _):
            at = pl.multiple_of(t * TILE, TILE)
            rows = pl.ds(at, TILE)
            total = [jnp.zeros((TILE, 2 * half), F32)] * 2
            for ch in range(chans):
                re = m_v[d, 0, ch, rows, :].astype(F32)
                im = m_v[d, 1, ch, rows, :].astype(F32)
                sq = (re * re + im * im) * w_v[ch, rows, :].astype(F32)
                second = idx[d, ch].astype(F32)
                part = sq * second
                total = [total[0] + sq, total[1] + part]
            out = pl.ds(pl.multiple_of(l * half + at, TILE), TILE)
            d_v[core, out, :] = (total[0] - total[1]).astype(BF16)
            d_v[2 + core, out, :] = total[1].astype(BF16)
            return 0

        lax.fori_loop(0, half // TILE, tile, 0)

    local[4].wait()
    for l in range(2):
        squares(e, l)

    gains_sib.wait_recv()
    for s in range(2):
        for x in range(2):
            for l in range(2):
                for k in range(2):
                    at = k * 8 + x * 4 + s * 2 + l
                    g_c[at : at + 1, :] = gin_c[s, x, l, k : k + 1, :]

    for l in range(2):
        remote(
            model.at[l, :, :, theirs, :], m_v.at[2 * other + l], mod_s.at[l], mod_r.at[l], sib
        ).wait_recv()
        squares(other, l)

    @pl.when(near)
    def _():
        gin_r[...] = gin_c[...]

    @pl.when(jnp.logical_not(near))
    def _():
        for s in range(2):
            remote(gin_c.at[s], gin_r.at[s], gr_s.at[0], gr_r.at[s], sib).wait_recv()

    lanes = pl.ds(pl.multiple_of(e * half, half), half)
    for s in range(2):
        for x in range(2):
            for l in range(2):
                for k in range(2):
                    at = k * 8 + x * 4 + s * 2 + l
                    g_r[at : at + 1, :] = gin_r[s, x, l, k : k + 1, lanes]
    local[5].wait()

    def sweep(step):
        gr, gc = g_r[...], g_c[...]
        outer_products(a_v, gr, gc)

        def channel(ch, _):
            picks = [idx[d, ch] for d in range(4)]
            before = [prev[d, ch] for d in range(4)]
            for t in range(half // TILE):
                rows = slice(t * TILE, (t + 1) * TILE)
                below = slice(half + t * TILE, half + (t + 1) * TILE)
                re, im = residual_tile(a_v, m_v, v_v, ch, picks, rows)
                w = w_v[ch, rows, :]
                re = re.astype(BF16) * w
                im = im.astype(BF16) * w
                for d in range(4):
                    m_re = m_v[d, 0, ch, rows, :]
                    m_im = m_v[d, 1, ch, rows, :]
                    old_re = t_v[before[d], d, rows, :]
                    old_im = t_v[before[d], d, below, :]
                    t_v[ch, d, rows, :] = old_re + (re * m_re + im * m_im)
                    t_v[ch, d, below, :] = old_im + (re * m_im - im * m_re)
            return 0

        lax.fori_loop(0, chans, channel, 0)
        x_col = jnp.concatenate([gr, turned(gr)], axis=1).astype(BF16)
        x_row = gc.astype(BF16)
        at16 = rows_like((16, 2 * half))
        o_col = jnp.zeros((16, 2 * half), F32)
        o_row = jnp.zeros((16, 2 * half), F32)
        for k in range(2):
            for d in range(4):
                keep = (at16 == 8 * k + d) | (at16 == 8 * k + 4 + d)
                part = t_v[last[k, d], d]
                got = jnp.dot(x_col, part, preferred_element_type=F32)
                o_col = jnp.where(keep, got, o_col)
                got = lax.dot_general(
                    x_row, part, (((1,), (1,)), ((), ())), preferred_element_type=F32
                )
                o_row = jnp.where(keep, got, o_row)
        o_row = o_row[:, :half] - turned(o_row[:, half:])

        def squared(g):
            return jnp.concatenate(
                [g[8 * k : 8 * k + 4] ** 2 + g[8 * k + 4 : 8 * k + 8] ** 2 for k in range(2)],
                axis=0,
            )

        s_r, s_c = squared(gr), squared(gc).astype(BF16)
        at8 = rows_like(s_r.shape)
        den_c = jnp.zeros((8, 2 * half), F32)
        den_r = jnp.zeros((8, half), F32)
        for k in range(2):
            for pair in range(2):
                first = k * 4 + 2 * pair
                left = jnp.concatenate(
                    [jnp.where(at8 == first + i, s_r, 0.0) for i in range(2)], axis=1
                ).astype(BF16)
                part = d_v[k * 2 + pair]
                den_c += jnp.dot(left, part, preferred_element_type=F32)
                got = lax.dot_general(
                    s_c, part, (((1,), (1,)), ((), ())), preferred_element_type=F32
                )
                for i in range(2):
                    den_r = jnp.where(at8 == first + i, got[:, i * half : (i + 1) * half], den_r)
        colb[step, r] = jnp.concatenate([o_col, den_c], axis=0)
        rowb[step, c] = jnp.concatenate([o_row, den_r], axis=0)
        copies = []
        for k in row_list:
            copies.append(remote(
                colb.at[step, r], colb.at[step, r], col_s.at[step, k], col_r.at[step, r],
                row_peer(k),
            ))
        for k in col_list:
            copies.append(remote(
                rowb.at[step, c], rowb.at[step, c], row_s.at[step, k], row_r.at[step, c],
                col_peer(k),
            ))
        for cp in copies:
            cp.start()

        def refresh(g, total):
            den = total[16:24] + 1.0
            den = jnp.concatenate([den[0:4], den[0:4], den[4:8], den[4:8]], axis=0)
            return g + 0.5 * total[0:16] / den

        for k in row_list:
            src = lax.rem(r + k, n_row)
            remote(
                colb.at[step, src], colb.at[step, src], col_s.at[step, k], col_r.at[step, src],
                row_peer(k),
            ).wait_recv()
        total = colb[step, 0]
        for i in range(1, n_row):
            total = total + colb[step, i]
        colt[step, e] = total
        both = remote(
            colt.at[step, e], colt.at[step, e], ct_s.at[step], ct_r.at[step, e], sib
        )
        both.start()
        copies.append(both)
        for k in col_list:
            src = lax.rem(c + k, n_col)
            remote(
                rowb.at[step, src], rowb.at[step, src], row_s.at[step, k], row_r.at[step, src],
                col_peer(k),
            ).wait_recv()
        total = rowb[step, 0]
        for i in range(1, n_col):
            total = total + rowb[step, i]
        g_r[...] = refresh(gr, total)
        if step == ITERS - 1:
            g_r2[e] = g_r[...]
            rows_sib = remote(g_r2.at[e], g_r2.at[e], fin_s, fin_r.at[e], sib)
            rows_sib.start()
            copies.append(rows_sib)
        remote(
            colt.at[step, other], colt.at[step, other], ct_s.at[step], ct_r.at[step, other], sib
        ).wait_recv()
        g_c[...] = refresh(gc, colt[step, 0] + colt[step, 1])
        return copies

    copies = []
    for step in range(ITERS):
        copies += sweep(step)

    for cp in local[6:]:
        cp.wait()
    remote(
        model.at[:, :, their_ch, mine, :], mf_v.at[pl.ds(2 * other, 2)],
        mod_s.at[2], mod_r.at[2], sib,
    ).wait_recv()
    remote(g_r2.at[other], g_r2.at[other], fin_s, fin_r.at[other], sib).wait_recv()

    for cp in model_a + [model_b, gains_sib]:
        cp.wait_send()

    @pl.when(near)
    def _():
        for cp in gains_to(near_to):
            cp.wait_send()

    @pl.when(cross)
    def _():
        for cp in gains_to(cross_to):
            cp.wait_send()

    for cp in copies:
        cp.wait_send()


def finish_kernel(m_v, v_v, mf_v, vf_v, g_r2, g_c, idx, gains_out, res_out, a_v, out_v, g_v, sem, g_sem):
    e = lax.axis_index("dir")
    half = m_v.shape[3]
    fin = mf_v.shape[2]
    g = g_c[...]
    for x in range(2):
        for l in range(2):
            for k in range(2):
                at = k * 8 + x * 4 + l
                g_v[x, l, k : k + 1, :] = jnp.where(e == 0, g[at : at + 1], g[at + 2 : at + 3])
    gains_copy = pltpu.make_async_copy(g_v, gains_out, g_sem)
    gains_copy.start()
    sides = (
        (m_v, v_v, e * fin, e),
        (mf_v, vf_v, 0, 1 - e),
    )

    def moved(which, ch):
        side = sides[which][3]
        where = pl.ds(pl.multiple_of(side * half, half), half)
        return pltpu.make_async_copy(
            out_v.at[which, :, ch], res_out.at[:, ch, where, :], sem.at[which, ch]
        )

    for which, (mod, vi, base, side) in enumerate(sides):
        outer_products(a_v.at[which], g_r2[side], g)

        def channel(ch, _):
            picks = [idx[d, e * fin + ch] for d in range(4)]
            for t in range(half // TILE):
                rows = slice(t * TILE, (t + 1) * TILE)
                re, im = residual_tile(a_v.at[which], mod, vi, base + ch, picks, rows)
                out_v[which, 0, ch, rows, :] = re
                out_v[which, 1, ch, rows, :] = im
            moved(which, ch).start()
            return 0

        lax.fori_loop(0, fin, channel, 0)
    gains_copy.wait()
    for which in range(2):
        for ch in range(fin):
            moved(which, ch).wait()


def body(n_row, n_col, vis, model, gains, channel_interval_index, antenna_usable_mask):
    dirs, _, chans, rows, cols = model.shape
    half = rows // 2
    fin = chans // 2
    n_dir = 2 * dirs
    hbm = pl.BlockSpec(memory_space=pltpu.HBM)
    vmem = pl.BlockSpec(memory_space=pltpu.VMEM)
    smem = pl.BlockSpec(memory_space=pltpu.SMEM)
    dma = pltpu.SemaphoreType.DMA
    held = (
        pltpu.VMEM((n_dir, 2, chans, half, cols), BF16),
        pltpu.VMEM((2, chans, half, cols), BF16),
        pltpu.VMEM((n_dir, 2, fin, half, cols), BF16),
        pltpu.VMEM((2, fin, half, cols), BF16),
        pltpu.VMEM((2, 16, half), F32),
        pltpu.VMEM((16, cols), F32),
        pltpu.SMEM((n_dir, chans), jnp.int32),
    )
    spaces = (vmem,) * 6 + (smem,)
    args = [
        pltpu.with_memory_space_constraint(x, pltpu.HBM)
        for x in (vis, model, gains, antenna_usable_mask, channel_interval_index)
    ]
    state = pl.pallas_call(
        functools.partial(kernel, n_row, n_col),
        out_shape=held,
        in_specs=[hbm] * 5,
        out_specs=spaces,
        scratch_shapes=[
            pltpu.VMEM((chans, half, cols), BF16),
            pltpu.VMEM((4, 2 * half, cols), BF16),
            pltpu.VMEM((8, half, 2 * cols), F32),
            pltpu.VMEM((chans + 1, n_dir, 2 * half, cols), BF16),
            pltpu.VMEM((chans, half), jnp.int32),
            pltpu.VMEM((chans, cols), jnp.int32),
            pltpu.SMEM((n_dir, chans), jnp.int32),
            pltpu.SMEM((2, n_dir), jnp.int32),
            pltpu.VMEM((2,) + gains.shape, F32),
            pltpu.VMEM((2,) + gains.shape, F32),
            pltpu.VMEM((16, half), F32),
            pltpu.VMEM((ITERS, n_row, 24, cols), F32),
            pltpu.VMEM((ITERS, n_col, 24, half), F32),
            pltpu.VMEM((ITERS, 2, 24, cols), F32),
            dma((8,)),
            dma((3,)),
            dma((3,)),
            dma,
            dma,
            dma((n_col,)),
            dma((2,)),
            dma((ITERS, n_row)),
            dma((ITERS, n_row)),
            dma((ITERS, n_col)),
            dma((ITERS, n_col)),
            dma((ITERS,)),
            dma((ITERS, 2)),
            dma,
            dma((2,)),
        ],
        compiler_params=pltpu.CompilerParams(
            collective_id=0, has_side_effects=True, vmem_limit_bytes=24 * 2**20
        ),
    )(*args)
    return pl.pallas_call(
        finish_kernel,
        out_shape=(
            pltpu.HBM(gains.shape, F32),
            pltpu.HBM((2, fin, rows, cols), F32),
        ),
        in_specs=spaces,
        out_specs=(hbm, hbm),
        scratch_shapes=[
            pltpu.VMEM((2, 8, half, 2 * cols), F32),
            pltpu.VMEM((2, 2, fin, half, cols), F32),
            pltpu.VMEM(gains.shape, F32),
            dma((2, fin)),
            dma,
        ],
        compiler_params=pltpu.CompilerParams(vmem_limit_bytes=16 * 2**20),
    )(*state)


def solution(mesh):
    placed = (
        P(None, None, "row", "col"),
        P("dir", None, None, "row", "col"),
        P(None, "dir", None, "col"),
        P(),
        P(),
    )
    return jax.shard_map(
        functools.partial(body, mesh.shape["row"], mesh.shape["col"]),
        mesh=mesh,
        in_specs=placed,
        out_specs=(P(None, "dir", None, "col"), P(None, "dir", "row", "col")),
        check_vma=False,
    )
```

```python
import functools

import jax
import jax.numpy as jnp
from jax import lax
from jax.experimental import pallas as pl
from jax.experimental.pallas import tpu as pltpu
from jax.sharding import PartitionSpec as P

ITERS = 2
MESH = pl.DeviceIdType.MESH
F32, BF16 = jnp.float32, jnp.bfloat16
TILE = 16


def rows_like(shape):
    return lax.broadcasted_iota(jnp.int32, shape, 0)


def turned(g):
    count = g.shape[0] // 8
    out = []
    for k in range(count):
        out += [-g[8 * k + 4 : 8 * k + 8], g[8 * k : 8 * k + 4]]
    return jnp.concatenate(out, axis=0)


def halves(x):
    high = x.astype(BF16)
    return high, (x - high.astype(F32)).astype(BF16)


def outer_products(a_ref, g_rows, g_cols):
    width = g_cols.shape[1]
    right = jnp.concatenate([g_cols, turned(g_cols)], axis=1)
    right_hi, right_lo = halves(right)
    right_all = jnp.concatenate([right_hi, right_lo, right_hi], axis=0).astype(F32)
    left_hi, left_lo = halves(g_rows)
    left = jnp.concatenate([left_hi, left_hi, left_lo], axis=0).astype(F32).T.astype(BF16)
    at = rows_like(right_all.shape) % 16
    for k in range(2):
        for d in range(4):
            keep = (at == 8 * k + d) | (at == 8 * k + 4 + d)
            a_ref[k * 4 + d] = jnp.dot(
                left, jnp.where(keep, right_all, 0.0).astype(BF16), preferred_element_type=F32
            )


def residual_tile(a, mod, vi, ch, picks, rows):
    re = vi[0, ch, rows, :].astype(F32)
    im = vi[1, ch, rows, :].astype(F32)
    width = re.shape[1]
    for d in range(4):
        at = picks[d] * 4 + d
        a_re = a[at, rows, 0:width]
        a_im = a[at, rows, width : 2 * width]
        m_re = mod[d, 0, ch, rows, :].astype(F32)
        m_im = mod[d, 1, ch, rows, :].astype(F32)
        re = re - a_re * m_re + a_im * m_im
        im = im - a_re * m_im - a_im * m_re
    return re, im


def kernel(
    n_row, n_col,
    vis, model, gains, mask, index,
    m_v, v_v, mf_v, vf_v, g_r2, g_c, idx,
    w_v, d_v, a_v, t_v, fri_v, fci_v, prev, last,
    gin_c, gin_r, g_r, coln, cold, rown, rowd, colt,
    loc_sem, mod_s, mod_r, gs_s, gs_r, gr_s, gr_r,
    cn_s, cn_r, cd_s, cd_r, rn_s, rn_r, rd_s, rd_r, ct_s, ct_r, fin_s, fin_r,
):
    r, c, e = lax.axis_index("row"), lax.axis_index("col"), lax.axis_index("dir")
    other = 1 - e
    sib = (r, c, other)
    half = model.shape[3] // 2
    chans = model.shape[2]
    fin = chans // 2
    quad = n_col // 2

    def row_peer(k):
        return lax.rem(r + k, n_row), c, e

    def col_peer(k):
        return r, lax.rem(c + k, n_col), e

    row_list = sorted(range(1, n_row), key=lambda k: (k % 2 == 0, abs(k - n_row // 2)))
    col_list = sorted(range(1, n_col), key=lambda k: abs(k - n_col // 2))

    flip_r = r + 1 - 2 * lax.rem(r, 2)
    flip_c = c + 1 - 2 * lax.rem(c, 2)
    near = r == c
    cross = r == flip_c
    same = lax.div(r, quad) == lax.div(c, quad)
    source_row = jnp.where(same, r, flip_r)
    near_to = [
        (r, lax.div(c, quad) * quad + lax.rem(c + k, quad), x)
        for k in range(1, quad) for x in range(2)
    ]
    cross_to = [
        (c, (1 - lax.div(c, quad)) * quad + k, x) for k in range(quad) for x in range(2)
    ]

    barrier = pltpu.get_barrier_semaphore()

    @pl.when(jnp.logical_not(near))
    def _():
        for x in range(2):
            pl.semaphore_signal(
                barrier, inc=1, device_id=(source_row, r, x), device_id_type=MESH
            )

    for k in col_list:
        pl.semaphore_signal(barrier, inc=1, device_id=col_peer(k), device_id_type=MESH)
    for k in row_list:
        pl.semaphore_signal(barrier, inc=1, device_id=row_peer(k), device_id_type=MESH)
    pl.semaphore_signal(barrier, inc=1, device_id=sib, device_id_type=MESH)

    mine = pl.ds(pl.multiple_of(e * half, half), half)
    theirs = pl.ds(pl.multiple_of(other * half, half), half)
    my_ch = pl.ds(e * fin, fin)
    their_ch = pl.ds(other * fin, fin)
    block_r = pl.ds(pl.multiple_of(r * 2 * half + e * half, half), half)
    block_c = pl.ds(pl.multiple_of(c * 2 * half, 2 * half), 2 * half)
    own_dirs = pl.ds(2 * e, 2)
    local = [
        (gains, gin_c.at[e]),
        (index, idx),
        (mask.at[:, block_r], fri_v),
        (mask.at[:, block_c], fci_v),
        (model.at[:, :, :, mine, :], m_v.at[own_dirs]),
        (vis.at[:, :, mine, :], v_v),
        (vis.at[:, my_ch, theirs, :], vf_v),
        (model.at[:, :, my_ch, theirs, :], mf_v.at[own_dirs]),
    ]
    local = [pltpu.make_async_copy(s, d, loc_sem.at[i]) for i, (s, d) in enumerate(local)]
    for cp in local:
        cp.start()

    def remote(src, dst, send, recv, device):
        return pltpu.make_async_remote_copy(
            src_ref=src, dst_ref=dst, send_sem=send, recv_sem=recv,
            device_id=device, device_id_type=MESH,
        )

    local[0].wait()
    n_near, n_cross = len(near_to), len(cross_to)
    pl.semaphore_wait(
        barrier,
        len(col_list) + len(row_list) + 1
        + jnp.where(near, n_near, 0) + jnp.where(cross, n_cross, 0),
    )

    def gains_to(devices):
        return [
            remote(gin_c.at[e], gin_r.at[e], gr_s.at[i], gr_r.at[e], to)
            for i, to in enumerate(devices)
        ]

    @pl.when(near)
    def _():
        for cp in gains_to(near_to):
            cp.start()

    @pl.when(cross)
    def _():
        for cp in gains_to(cross_to):
            cp.start()

    gains_sib = remote(gin_c.at[e], gin_c.at[e], gs_s, gs_r, sib)
    gains_sib.start()

    def chunk(ch, dirs):
        return remote(
            model.at[:, :, ch, theirs, :], m_v.at[dirs, :, ch], mod_s.at[ch], mod_r.at[ch], sib
        )

    model_a = [chunk(ch, own_dirs) for ch in range(chans)]
    model_b = remote(
        model.at[:, :, their_ch, mine, :], mf_v.at[own_dirs],
        mod_s.at[chans], mod_r.at[chans], sib,
    )
    for cp in model_a:
        cp.start()
    model_b.start()

    for cp in local[1:4]:
        cp.wait()
    for d in range(4):
        ends = [jnp.int32(chans), jnp.int32(chans)]
        for ch in range(chans):
            second = idx[d, ch] == 1
            prev[d, ch] = jnp.where(second, ends[1], ends[0])
            ends = [jnp.where(second, ends[0], ch), jnp.where(second, ch, ends[1])]
        for k in range(2):
            last[k, d] = ends[k]
    t_v[chans] = jnp.zeros(t_v.shape[1:], BF16)
    shape = (half, 2 * half)
    p_at = r * 2 * half + e * half + rows_like(shape)
    q_at = c * 2 * half + lax.broadcasted_iota(jnp.int32, shape, 1)
    apart = p_at != q_at
    f_r = fri_v[...].astype(F32)
    f_c = fci_v[...].astype(F32).astype(BF16)
    for ch in range(chans):
        one = jnp.where(rows_like(f_r.shape) == ch, f_r, 0.0).astype(BF16)
        both = lax.dot_general(
            one, f_c, (((0,), (0,)), ((), ())), preferred_element_type=F32
        )
        w_v[ch] = jnp.where(apart, both, 0.0).astype(BF16)

    def squares(core, l):
        d = 2 * core + l

        def tile(t, _):
            at = pl.multiple_of(t * TILE, TILE)
            rows = pl.ds(at, TILE)
            total = [jnp.zeros((TILE, 2 * half), F32)] * 2
            for ch in range(chans):
                re = m_v[d, 0, ch, rows, :].astype(F32)
                im = m_v[d, 1, ch, rows, :].astype(F32)
                sq = (re * re + im * im) * w_v[ch, rows, :].astype(F32)
                second = idx[d, ch].astype(F32)
                part = sq * second
                total = [total[0] + sq, total[1] + part]
            out = pl.ds(pl.multiple_of(l * half + at, TILE), TILE)
            d_v[core, out, :] = (total[0] - total[1]).astype(BF16)
            d_v[2 + core, out, :] = total[1].astype(BF16)
            return 0

        lax.fori_loop(0, half // TILE, tile, 0)

    local[4].wait()
    for l in range(2):
        squares(e, l)

    gains_sib.wait_recv()
    for s in range(2):
        for x in range(2):
            for l in range(2):
                for k in range(2):
                    at = k * 8 + x * 4 + s * 2 + l
                    g_c[at : at + 1, :] = gin_c[s, x, l, k : k + 1, :]

    @pl.when(near)
    def _():
        gin_r[...] = gin_c[...]

    @pl.when(jnp.logical_not(near))
    def _():
        for s in range(2):
            remote(gin_c.at[s], gin_r.at[s], gr_s.at[0], gr_r.at[s], sib).wait_recv()

    lanes = pl.ds(pl.multiple_of(e * half, half), half)
    for s in range(2):
        for x in range(2):
            for l in range(2):
                for k in range(2):
                    at = k * 8 + x * 4 + s * 2 + l
                    g_r[at : at + 1, :] = gin_r[s, x, l, k : k + 1, lanes]
    local[5].wait()

    def sweep(step):
        gr, gc = g_r[...], g_c[...]
        at16 = rows_like((16, 2 * half))
        at8 = rows_like((8, half))
        copies = []

        def send(buf, at, sems, ks, peer):
            for k in ks:
                cp = remote(
                    buf.at[step, at], buf.at[step, at], sems[0].at[step, k],
                    sems[1].at[step, at], peer(k),
                )
                cp.start()
                copies.append(cp)

        def gathered(buf, sems, at, count, ks, peer):
            for k in ks:
                src = lax.rem(at + k, count)
                remote(
                    buf.at[step, src], buf.at[step, src], sems[0].at[step, k],
                    sems[1].at[step, src], peer(k),
                ).wait_recv()
            total = buf[step, 0]
            for i in range(1, count):
                total = total + buf[step, i]
            return total

        def across(g, part):
            return lax.dot_general(g, part, (((1,), (1,)), ((), ())), preferred_element_type=F32)

        def squared(g):
            return jnp.concatenate(
                [g[8 * k : 8 * k + 4] ** 2 + g[8 * k + 4 : 8 * k + 8] ** 2 for k in range(2)],
                axis=0,
            )

        def denominators():
            s_r = squared(gr)
            s_c = squared(gc).astype(BF16)
            den_c = jnp.zeros((8, 2 * half), F32)
            den_r = jnp.zeros((8, half), F32)
            for k in range(2):
                for pair in range(2):
                    first = k * 4 + 2 * pair
                    left = jnp.concatenate(
                        [jnp.where(at8 == first + i, s_r, 0.0) for i in range(2)], axis=1
                    ).astype(BF16)
                    part = d_v[k * 2 + pair]
                    den_c += jnp.dot(left, part, preferred_element_type=F32)
                    got = across(s_c, part)
                    for i in range(2):
                        den_r = jnp.where(
                            at8 == first + i, got[:, i * half : (i + 1) * half], den_r
                        )
            rowd[step, c] = den_r
            send(rowd, c, (rd_s, rd_r), col_list, col_peer)
            cold[step, r] = den_c
            send(cold, r, (cd_s, cd_r), row_list, row_peer)

        def channel(ch, _):
            if step == 0:
                chunk(ch, pl.ds(2 * other, 2)).wait_recv()
            picks = [idx[d, ch] for d in range(4)]
            before = [prev[d, ch] for d in range(4)]
            for t in range(half // TILE):
                rows = slice(t * TILE, (t + 1) * TILE)
                below = slice(half + t * TILE, half + (t + 1) * TILE)
                re, im = residual_tile(a_v, m_v, v_v, ch, picks, rows)
                w = w_v[ch, rows, :]
                re = re.astype(BF16) * w
                im = im.astype(BF16) * w
                for d in range(4):
                    m_re = m_v[d, 0, ch, rows, :]
                    m_im = m_v[d, 1, ch, rows, :]
                    old_re = t_v[before[d], d, rows, :]
                    old_im = t_v[before[d], d, below, :]
                    t_v[ch, d, rows, :] = old_re + (re * m_re + im * m_im)
                    t_v[ch, d, below, :] = old_im + (re * m_im - im * m_re)
            return 0

        def all_parts(product):
            out = jnp.zeros((16, 2 * half), F32)
            for k in range(2):
                for d in range(4):
                    keep = (at16 == 8 * k + d) | (at16 == 8 * k + 4 + d)
                    out = jnp.where(keep, product(t_v[last[k, d], d]), out)
            return out

        if step > 0:
            denominators()
        outer_products(a_v, gr, gc)
        lax.fori_loop(0, chans, channel, 0)
        x_row = gc.astype(BF16)
        x_col = jnp.concatenate([gr, turned(gr)], axis=1).astype(BF16)
        o_row = all_parts(lambda part: across(x_row, part))
        rown[step, c] = o_row[:, :half] - turned(o_row[:, half:])
        send(rown, c, (rn_s, rn_r), col_list, col_peer)
        coln[step, r] = all_parts(
            lambda part: jnp.dot(x_col, part, preferred_element_type=F32)
        )
        send(coln, r, (cn_s, cn_r), row_list, row_peer)
        if step == 0:
            for l in range(2):
                squares(other, l)
            denominators()

        def refresh(g, total, den):
            den = den + 1.0
            den = jnp.concatenate([den[0:4], den[0:4], den[4:8], den[4:8]], axis=0)
            return g + 0.5 * total / den

        total = gathered(coln, (cn_s, cn_r), r, n_row, row_list, row_peer)
        total_den = gathered(cold, (cd_s, cd_r), r, n_row, row_list, row_peer)
        colt[step, e] = jnp.concatenate([total, total_den], axis=0)
        both = remote(
            colt.at[step, e], colt.at[step, e], ct_s.at[step], ct_r.at[step, e], sib
        )
        both.start()
        copies.append(both)
        total = gathered(rown, (rn_s, rn_r), c, n_col, col_list, col_peer)
        total_den = gathered(rowd, (rd_s, rd_r), c, n_col, col_list, col_peer)
        g_r[...] = refresh(gr, total, total_den)
        if step == ITERS - 1:
            g_r2[e] = g_r[...]
            rows_sib = remote(g_r2.at[e], g_r2.at[e], fin_s, fin_r.at[e], sib)
            rows_sib.start()
            copies.append(rows_sib)
        remote(
            colt.at[step, other], colt.at[step, other], ct_s.at[step], ct_r.at[step, other], sib
        ).wait_recv()
        total = colt[step, 0] + colt[step, 1]
        g_c[...] = refresh(gc, total[0:16], total[16:24])
        return copies

    copies = []
    for step in range(ITERS):
        copies += sweep(step)

    for cp in local[6:]:
        cp.wait()
    remote(
        model.at[:, :, their_ch, mine, :], mf_v.at[pl.ds(2 * other, 2)],
        mod_s.at[chans], mod_r.at[chans], sib,
    ).wait_recv()
    remote(g_r2.at[other], g_r2.at[other], fin_s, fin_r.at[other], sib).wait_recv()

    for cp in model_a + [model_b, gains_sib]:
        cp.wait_send()

    @pl.when(near)
    def _():
        for cp in gains_to(near_to):
            cp.wait_send()

    @pl.when(cross)
    def _():
        for cp in gains_to(cross_to):
            cp.wait_send()

    for cp in copies:
        cp.wait_send()


def finish_kernel(m_v, v_v, mf_v, vf_v, g_r2, g_c, idx, gains_out, res_out, a_v, out_v, g_v, sem, g_sem):
    e = lax.axis_index("dir")
    half = m_v.shape[3]
    fin = mf_v.shape[2]
    g = g_c[...]
    for x in range(2):
        for l in range(2):
            for k in range(2):
                at = k * 8 + x * 4 + l
                g_v[x, l, k : k + 1, :] = jnp.where(e == 0, g[at : at + 1], g[at + 2 : at + 3])
    gains_copy = pltpu.make_async_copy(g_v, gains_out, g_sem)
    gains_copy.start()
    sides = (
        (m_v, v_v, e * fin, e),
        (mf_v, vf_v, 0, 1 - e),
    )

    def moved(which, ch):
        side = sides[which][3]
        where = pl.ds(pl.multiple_of(side * half, half), half)
        return pltpu.make_async_copy(
            out_v.at[which, :, ch], res_out.at[:, ch, where, :], sem.at[which, ch]
        )

    for which, (mod, vi, base, side) in enumerate(sides):
        outer_products(a_v.at[which], g_r2[side], g)

        def channel(ch, _):
            picks = [idx[d, e * fin + ch] for d in range(4)]
            for t in range(half // TILE):
                rows = slice(t * TILE, (t + 1) * TILE)
                re, im = residual_tile(a_v.at[which], mod, vi, base + ch, picks, rows)
                out_v[which, 0, ch, rows, :] = re
                out_v[which, 1, ch, rows, :] = im
            moved(which, ch).start()
            return 0

        lax.fori_loop(0, fin, channel, 0)
    gains_copy.wait()
    for which in range(2):
        for ch in range(fin):
            moved(which, ch).wait()


def body(n_row, n_col, vis, model, gains, channel_interval_index, antenna_usable_mask):
    dirs, _, chans, rows, cols = model.shape
    half = rows // 2
    fin = chans // 2
    n_dir = 2 * dirs
    hbm = pl.BlockSpec(memory_space=pltpu.HBM)
    vmem = pl.BlockSpec(memory_space=pltpu.VMEM)
    smem = pl.BlockSpec(memory_space=pltpu.SMEM)
    dma = pltpu.SemaphoreType.DMA
    held = (
        pltpu.VMEM((n_dir, 2, chans, half, cols), BF16),
        pltpu.VMEM((2, chans, half, cols), BF16),
        pltpu.VMEM((n_dir, 2, fin, half, cols), BF16),
        pltpu.VMEM((2, fin, half, cols), BF16),
        pltpu.VMEM((2, 16, half), F32),
        pltpu.VMEM((16, cols), F32),
        pltpu.SMEM((n_dir, chans), jnp.int32),
    )
    spaces = (vmem,) * 6 + (smem,)
    args = [
        pltpu.with_memory_space_constraint(x, pltpu.HBM)
        for x in (vis, model, gains, antenna_usable_mask, channel_interval_index)
    ]
    state = pl.pallas_call(
        functools.partial(kernel, n_row, n_col),
        out_shape=held,
        in_specs=[hbm] * 5,
        out_specs=spaces,
        scratch_shapes=[
            pltpu.VMEM((chans, half, cols), BF16),
            pltpu.VMEM((4, 2 * half, cols), BF16),
            pltpu.VMEM((8, half, 2 * cols), F32),
            pltpu.VMEM((chans + 1, n_dir, 2 * half, cols), BF16),
            pltpu.VMEM((chans, half), jnp.int32),
            pltpu.VMEM((chans, cols), jnp.int32),
            pltpu.SMEM((n_dir, chans), jnp.int32),
            pltpu.SMEM((2, n_dir), jnp.int32),
            pltpu.VMEM((2,) + gains.shape, F32),
            pltpu.VMEM((2,) + gains.shape, F32),
            pltpu.VMEM((16, half), F32),
            pltpu.VMEM((ITERS, n_row, 16, cols), F32),
            pltpu.VMEM((ITERS, n_row, 8, cols), F32),
            pltpu.VMEM((ITERS, n_col, 16, half), F32),
            pltpu.VMEM((ITERS, n_col, 8, half), F32),
            pltpu.VMEM((ITERS, 2, 24, cols), F32),
            dma((8,)),
            dma((chans + 1,)),
            dma((chans + 1,)),
            dma,
            dma,
            dma((n_col,)),
            dma((2,)),
            dma((ITERS, n_row)),
            dma((ITERS, n_row)),
            dma((ITERS, n_row)),
            dma((ITERS, n_row)),
            dma((ITERS, n_col)),
            dma((ITERS, n_col)),
            dma((ITERS, n_col)),
            dma((ITERS, n_col)),
            dma((ITERS,)),
            dma((ITERS, 2)),
            dma,
            dma((2,)),
        ],
        compiler_params=pltpu.CompilerParams(
            collective_id=0, has_side_effects=True, vmem_limit_bytes=24 * 2**20
        ),
    )(*args)
    return pl.pallas_call(
        finish_kernel,
        out_shape=(
            pltpu.HBM(gains.shape, F32),
            pltpu.HBM((2, fin, rows, cols), F32),
        ),
        in_specs=spaces,
        out_specs=(hbm, hbm),
        scratch_shapes=[
            pltpu.VMEM((2, 8, half, 2 * cols), F32),
            pltpu.VMEM((2, 2, fin, half, cols), F32),
            pltpu.VMEM(gains.shape, F32),
            dma((2, fin)),
            dma,
        ],
        compiler_params=pltpu.CompilerParams(vmem_limit_bytes=16 * 2**20),
    )(*state)


def solution(mesh):
    placed = (
        P(None, None, "row", "col"),
        P("dir", None, None, "row", "col"),
        P(None, "dir", None, "col"),
        P(),
        P(),
    )
    return jax.shard_map(
        functools.partial(body, mesh.shape["row"], mesh.shape["col"]),
        mesh=mesh,
        in_specs=placed,
        out_specs=(P(None, "dir", None, "col"), P(None, "dir", "row", "col")),
        check_vma=False,
    )
```

```python
import functools

import jax
import jax.numpy as jnp
from jax import lax
from jax.experimental import pallas as pl
from jax.experimental.pallas import tpu as pltpu
from jax.sharding import PartitionSpec as P

ITERS = 2
MESH = pl.DeviceIdType.MESH
F32, BF16 = jnp.float32, jnp.bfloat16
TILE = 16


def rows_like(shape):
    return lax.broadcasted_iota(jnp.int32, shape, 0)


def turned(g):
    count = g.shape[0] // 8
    out = []
    for k in range(count):
        out += [-g[8 * k + 4 : 8 * k + 8], g[8 * k : 8 * k + 4]]
    return jnp.concatenate(out, axis=0)


def halves(x):
    high = x.astype(BF16)
    return high, (x - high.astype(F32)).astype(BF16)


def outer_products(a_ref, g_rows, g_cols):
    width = g_cols.shape[1]
    right = jnp.concatenate([g_cols, turned(g_cols)], axis=1)
    right_hi, right_lo = halves(right)
    right_all = jnp.concatenate([right_hi, right_lo, right_hi], axis=0).astype(F32)
    left_hi, left_lo = halves(g_rows)
    left = jnp.concatenate([left_hi, left_hi, left_lo], axis=0).astype(F32).T.astype(BF16)
    at = rows_like(right_all.shape) % 16
    for k in range(2):
        for d in range(4):
            keep = (at == 8 * k + d) | (at == 8 * k + 4 + d)
            a_ref[k * 4 + d] = jnp.dot(
                left, jnp.where(keep, right_all, 0.0).astype(BF16), preferred_element_type=F32
            )


def residual_tile(a, mod, vi, ch, picks, rows):
    re = vi[0, ch, rows, :].astype(F32)
    im = vi[1, ch, rows, :].astype(F32)
    width = re.shape[1]
    for d in range(4):
        at = picks[d] * 4 + d
        a_re = a[at, rows, 0:width]
        a_im = a[at, rows, width : 2 * width]
        m_re = mod[d, 0, ch, rows, :].astype(F32)
        m_im = mod[d, 1, ch, rows, :].astype(F32)
        re = re - a_re * m_re + a_im * m_im
        im = im - a_re * m_im - a_im * m_re
    return re, im


def kernel(
    n_row, n_col,
    vis, model, gains, mask, index,
    m_v, v_v, mf_v, vf_v, g_r2, g_c, idx,
    w_v, d_v, a_v, t_v, fri_v, fci_v, prev, last,
    gin_c, gin_r, g_r, coln, cold, rown, rowd, colns, colds, rowns, colt,
    late, loc_sem, mod_s, mod_r, gs_s, gs_r, gr_s, gr_r,
    cn_s, cn_r, cd_s, cd_r, rn_s, rn_r, rd_s, rd_r, ct_s, ct_r, fin_s, fin_r,
):
    r, c, e = lax.axis_index("row"), lax.axis_index("col"), lax.axis_index("dir")
    other = 1 - e
    sib = (r, c, other)
    half = model.shape[3] // 2
    chans = model.shape[2]
    fin = chans // 2
    quad = n_col // 2

    def row_peer(k):
        return lax.rem(r + k, n_row), c, e

    def col_peer(k):
        return r, lax.rem(c + k, n_col), e

    row_list = sorted(range(1, n_row), key=lambda k: (k % 2 == 0, abs(k - n_row // 2)))
    col_list = sorted(range(1, n_col), key=lambda k: abs(k - n_col // 2))

    flip_r = r + 1 - 2 * lax.rem(r, 2)
    flip_c = c + 1 - 2 * lax.rem(c, 2)
    near = r == c
    cross = r == flip_c
    same = lax.div(r, quad) == lax.div(c, quad)
    source_row = jnp.where(same, r, flip_r)
    near_to = [
        (r, lax.div(c, quad) * quad + lax.rem(c + k, quad), x)
        for k in range(1, quad) for x in range(2)
    ]
    cross_to = [
        (c, (1 - lax.div(c, quad)) * quad + k, x) for k in range(quad) for x in range(2)
    ]

    barrier = pltpu.get_barrier_semaphore()

    @pl.when(jnp.logical_not(near))
    def _():
        for x in range(2):
            pl.semaphore_signal(
                barrier, inc=1, device_id=(source_row, r, x), device_id_type=MESH
            )

    holder = near | cross
    partners = []
    for k in col_list:
        to = col_peer(k)
        partners.append((to, (to[1] == r) | (to[1] == flip_r)))
    for k in row_list:
        to = row_peer(k)
        partners.append((to, (to[0] == c) | (to[0] == flip_c)))
    for to, holds in partners:

        @pl.when(holder | jnp.logical_not(holds))
        def _(to=to):
            pl.semaphore_signal(barrier, inc=1, device_id=to, device_id_type=MESH)

    pl.semaphore_signal(barrier, inc=1, device_id=sib, device_id_type=MESH)

    mine = pl.ds(pl.multiple_of(e * half, half), half)
    theirs = pl.ds(pl.multiple_of(other * half, half), half)
    my_ch = pl.ds(e * fin, fin)
    their_ch = pl.ds(other * fin, fin)
    block_r = pl.ds(pl.multiple_of(r * 2 * half + e * half, half), half)
    block_c = pl.ds(pl.multiple_of(c * 2 * half, 2 * half), 2 * half)
    own_dirs = pl.ds(2 * e, 2)
    local = [
        (gains, gin_c.at[e]),
        (index, idx),
        (mask.at[:, block_r], fri_v),
        (mask.at[:, block_c], fci_v),
        (model.at[:, :, :, mine, :], m_v.at[own_dirs]),
        (vis.at[:, :, mine, :], v_v),
        (vis.at[:, my_ch, theirs, :], vf_v),
        (model.at[:, :, my_ch, theirs, :], mf_v.at[own_dirs]),
    ]
    local = [pltpu.make_async_copy(s, d, loc_sem.at[i]) for i, (s, d) in enumerate(local)]
    for cp in local:
        cp.start()

    def remote(src, dst, send, recv, device):
        return pltpu.make_async_remote_copy(
            src_ref=src, dst_ref=dst, send_sem=send, recv_sem=recv,
            device_id=device, device_id_type=MESH,
        )

    local[0].wait()
    n_near, n_cross = len(near_to), len(cross_to)
    pl.semaphore_wait(
        barrier,
        jnp.where(holder, 2, len(partners)) + 1
        + jnp.where(near, n_near, 0) + jnp.where(cross, n_cross, 0),
    )

    def gains_to(devices):
        return [
            remote(gin_c.at[e], gin_r.at[e], gr_s.at[i], gr_r.at[e], to)
            for i, to in enumerate(devices)
        ]

    @pl.when(near)
    def _():
        for cp in gains_to(near_to):
            cp.start()

    @pl.when(cross)
    def _():
        for cp in gains_to(cross_to):
            cp.start()

    gains_sib = remote(gin_c.at[e], gin_c.at[e], gs_s, gs_r, sib)
    gains_sib.start()

    def chunk(ch, dirs):
        return remote(
            model.at[:, :, ch, theirs, :], m_v.at[dirs, :, ch], mod_s.at[ch], mod_r.at[ch], sib
        )

    model_a = [chunk(ch, own_dirs) for ch in range(chans)]
    model_b = remote(
        model.at[:, :, their_ch, mine, :], mf_v.at[own_dirs],
        mod_s.at[chans], mod_r.at[chans], sib,
    )
    for cp in model_a:
        cp.start()
    model_b.start()

    for to, holds in partners:

        @pl.when(jnp.logical_not(holder) & holds)
        def _(to=to):
            pl.semaphore_signal(late, inc=1, device_id=to, device_id_type=MESH)

    for cp in local[1:4]:
        cp.wait()
    for d in range(4):
        ends = [jnp.int32(chans), jnp.int32(chans)]
        for ch in range(chans):
            second = idx[d, ch] == 1
            prev[d, ch] = jnp.where(second, ends[1], ends[0])
            ends = [jnp.where(second, ends[0], ch), jnp.where(second, ch, ends[1])]
        for k in range(2):
            last[k, d] = ends[k]
    t_v[chans] = jnp.zeros(t_v.shape[1:], BF16)
    shape = (half, 2 * half)
    p_at = r * 2 * half + e * half + rows_like(shape)
    q_at = c * 2 * half + lax.broadcasted_iota(jnp.int32, shape, 1)
    apart = p_at != q_at
    f_r = fri_v[...].astype(F32)
    f_c = fci_v[...].astype(F32).astype(BF16)
    for ch in range(chans):
        one = jnp.where(rows_like(f_r.shape) == ch, f_r, 0.0).astype(BF16)
        both = lax.dot_general(
            one, f_c, (((0,), (0,)), ((), ())), preferred_element_type=F32
        )
        w_v[ch] = jnp.where(apart, both, 0.0).astype(BF16)

    def squares(core, l):
        d = 2 * core + l

        def tile(t, _):
            at = pl.multiple_of(t * TILE, TILE)
            rows = pl.ds(at, TILE)
            total = [jnp.zeros((TILE, 2 * half), F32)] * 2
            for ch in range(chans):
                re = m_v[d, 0, ch, rows, :].astype(F32)
                im = m_v[d, 1, ch, rows, :].astype(F32)
                sq = (re * re + im * im) * w_v[ch, rows, :].astype(F32)
                second = idx[d, ch].astype(F32)
                part = sq * second
                total = [total[0] + sq, total[1] + part]
            out = pl.ds(pl.multiple_of(l * half + at, TILE), TILE)
            d_v[core, out, :] = (total[0] - total[1]).astype(BF16)
            d_v[2 + core, out, :] = total[1].astype(BF16)
            return 0

        lax.fori_loop(0, half // TILE, tile, 0)

    local[4].wait()
    for l in range(2):
        squares(e, l)

    gains_sib.wait_recv()
    for s in range(2):
        for x in range(2):
            for l in range(2):
                for k in range(2):
                    at = k * 8 + x * 4 + s * 2 + l
                    g_c[at : at + 1, :] = gin_c[s, x, l, k : k + 1, :]

    @pl.when(near)
    def _():
        gin_r[...] = gin_c[...]

    @pl.when(jnp.logical_not(near))
    def _():
        for s in range(2):
            remote(gin_c.at[s], gin_r.at[s], gr_s.at[0], gr_r.at[s], sib).wait_recv()

    lanes = pl.ds(pl.multiple_of(e * half, half), half)
    for s in range(2):
        for x in range(2):
            for l in range(2):
                for k in range(2):
                    at = k * 8 + x * 4 + s * 2 + l
                    g_r[at : at + 1, :] = gin_r[s, x, l, k : k + 1, lanes]
    local[5].wait()

    def sweep(step, error):
        gr, gc = g_r[...], g_c[...]
        short = step == 0
        at16 = rows_like((16, 2 * half))
        at8 = rows_like((8, half))
        copies = []

        def send(buf, at, sems, ks, peer):
            for k in ks:
                cp = remote(
                    buf.at[step, at], buf.at[step, at], sems[0].at[step, k],
                    sems[1].at[step, at], peer(k),
                )
                cp.start()
                copies.append(cp)

        def gathered(buf, sems, at, count, ks, peer):
            for k in ks:
                src = lax.rem(at + k, count)
                remote(
                    buf.at[step, src], buf.at[step, src], sems[0].at[step, k],
                    sems[1].at[step, src], peer(k),
                ).wait_recv()
            total = buf[step, 0].astype(F32)
            for i in range(1, count):
                total = total + buf[step, i].astype(F32)
            return total

        def across(g, part):
            return lax.dot_general(g, part, (((1,), (1,)), ((), ())), preferred_element_type=F32)

        def squared(g):
            return jnp.concatenate(
                [g[8 * k : 8 * k + 4] ** 2 + g[8 * k + 4 : 8 * k + 8] ** 2 for k in range(2)],
                axis=0,
            )

        def denominators():
            s_r = squared(gr)
            s_c = squared(gc).astype(BF16)
            den_c = jnp.zeros((8, 2 * half), F32)
            den_r = jnp.zeros((8, half), F32)
            for k in range(2):
                for pair in range(2):
                    first = k * 4 + 2 * pair
                    left = jnp.concatenate(
                        [jnp.where(at8 == first + i, s_r, 0.0) for i in range(2)], axis=1
                    ).astype(BF16)
                    part = d_v[k * 2 + pair]
                    den_c += jnp.dot(left, part, preferred_element_type=F32)
                    got = across(s_c, part)
                    for i in range(2):
                        den_r = jnp.where(
                            at8 == first + i, got[:, i * half : (i + 1) * half], den_r
                        )
            rowd[step, c] = den_r
            send(rowd, c, (rd_s, rd_r), col_list, col_peer)
            if short:
                den_16 = den_c.astype(BF16)
                colds[step, r] = jnp.concatenate([den_16[:, :half], den_16[:, half:]], axis=0)
                send(colds, r, (cd_s, cd_r), row_list, row_peer)
                return den_c - den_16.astype(F32)
            cold[step, r] = den_c
            send(cold, r, (cd_s, cd_r), row_list, row_peer)
            return None

        def channel(ch, _):
            if step == 0:
                chunk(ch, pl.ds(2 * other, 2)).wait_recv()
            picks = [idx[d, ch] for d in range(4)]
            before = [prev[d, ch] for d in range(4)]
            for t in range(half // TILE):
                rows = slice(t * TILE, (t + 1) * TILE)
                below = slice(half + t * TILE, half + (t + 1) * TILE)
                re, im = residual_tile(a_v, m_v, v_v, ch, picks, rows)
                w = w_v[ch, rows, :]
                re = re.astype(BF16) * w
                im = im.astype(BF16) * w
                for d in range(4):
                    m_re = m_v[d, 0, ch, rows, :]
                    m_im = m_v[d, 1, ch, rows, :]
                    old_re = t_v[before[d], d, rows, :]
                    old_im = t_v[before[d], d, below, :]
                    t_v[ch, d, rows, :] = old_re + (re * m_re + im * m_im)
                    t_v[ch, d, below, :] = old_im + (re * m_im - im * m_re)
            return 0

        def all_parts(product):
            out = jnp.zeros((16, 2 * half), F32)
            for k in range(2):
                for d in range(4):
                    keep = (at16 == 8 * k + d) | (at16 == 8 * k + 4 + d)
                    out = jnp.where(keep, product(t_v[last[k, d], d]), out)
            return out

        if step > 0:
            denominators()
        outer_products(a_v, gr, gc)
        lax.fori_loop(0, chans, channel, 0)
        if step == 0:

            @pl.when(holder)
            def _():
                pl.semaphore_wait(late, len(partners) - 2)

        x_row = gc.astype(BF16)
        x_col = jnp.concatenate([gr, turned(gr)], axis=1).astype(BF16)
        o_row = all_parts(lambda part: across(x_row, part))
        o_row = o_row[:, :half] - turned(o_row[:, half:])
        if short:
            rowns[step, c] = o_row.astype(BF16)
            send(rowns, c, (rn_s, rn_r), col_list, col_peer)
        else:
            rown[step, c] = o_row + error[0]
            send(rown, c, (rn_s, rn_r), col_list, col_peer)
        o_col = all_parts(lambda part: jnp.dot(x_col, part, preferred_element_type=F32))
        if short:
            colns[step, r] = o_col.astype(BF16)
            send(colns, r, (cn_s, cn_r), row_list, row_peer)
            for l in range(2):
                squares(other, l)
            lost_den = denominators()
        else:
            coln[step, r] = o_col + error[1]
            send(coln, r, (cn_s, cn_r), row_list, row_peer)

        def refresh(total, den):
            den = den + 1.0
            den = jnp.concatenate([den[0:4], den[0:4], den[4:8], den[4:8]], axis=0)
            return 0.5 * total / den

        total = gathered(colns if short else coln, (cn_s, cn_r), r, n_row, row_list, row_peer)
        total_den = gathered(colds if short else cold, (cd_s, cd_r), r, n_row, row_list, row_peer)
        if short:
            total_den = jnp.concatenate([total_den[0:8], total_den[8:16]], axis=1)
        colt[step, e] = jnp.concatenate([total, total_den], axis=0)
        both = remote(
            colt.at[step, e], colt.at[step, e], ct_s.at[step], ct_r.at[step, e], sib
        )
        both.start()
        copies.append(both)
        total = gathered(rowns if short else rown, (rn_s, rn_r), c, n_col, col_list, col_peer)
        total_den = gathered(rowd, (rd_s, rd_r), c, n_col, col_list, col_peer)
        change_r = refresh(total, total_den)
        g_r[...] = gr + change_r
        if step == ITERS - 1:
            g_r2[e] = g_r[...]
            rows_sib = remote(g_r2.at[e], g_r2.at[e], fin_s, fin_r.at[e], sib)
            rows_sib.start()
            copies.append(rows_sib)
        remote(
            colt.at[step, other], colt.at[step, other], ct_s.at[step], ct_r.at[step, other], sib
        ).wait_recv()
        total = colt[step, 0] + colt[step, 1]
        change_c = refresh(total[0:16], total[16:24])
        g_c[...] = gc + change_c
        if short:
            lost_r = o_row - rowns[step, c].astype(F32)
            lost_c = o_col - colns[step, r].astype(F32)
            lost_den = jnp.concatenate(
                [lost_den[0:4], lost_den[0:4], lost_den[4:8], lost_den[4:8]], axis=0
            )
            error = (0.5 * lost_r, 0.5 * lost_c - change_c * lost_den)
        return copies, error

    copies, error = [], None
    for step in range(ITERS):
        started, error = sweep(step, error)
        copies += started

    for cp in local[6:]:
        cp.wait()
    remote(
        model.at[:, :, their_ch, mine, :], mf_v.at[pl.ds(2 * other, 2)],
        mod_s.at[chans], mod_r.at[chans], sib,
    ).wait_recv()
    remote(g_r2.at[other], g_r2.at[other], fin_s, fin_r.at[other], sib).wait_recv()

    for cp in model_a + [model_b, gains_sib]:
        cp.wait_send()

    @pl.when(near)
    def _():
        for cp in gains_to(near_to):
            cp.wait_send()

    @pl.when(cross)
    def _():
        for cp in gains_to(cross_to):
            cp.wait_send()

    for cp in copies:
        cp.wait_send()


def finish_kernel(m_v, v_v, mf_v, vf_v, g_r2, g_c, idx, gains_out, res_out, a_v, out_v, g_v, sem, g_sem):
    e = lax.axis_index("dir")
    half = m_v.shape[3]
    fin = mf_v.shape[2]
    g = g_c[...]
    for x in range(2):
        for l in range(2):
            for k in range(2):
                at = k * 8 + x * 4 + l
                g_v[x, l, k : k + 1, :] = jnp.where(e == 0, g[at : at + 1], g[at + 2 : at + 3])
    gains_copy = pltpu.make_async_copy(g_v, gains_out, g_sem)
    gains_copy.start()
    sides = (
        (m_v, v_v, e * fin, e),
        (mf_v, vf_v, 0, 1 - e),
    )

    def moved(which, ch):
        side = sides[which][3]
        where = pl.ds(pl.multiple_of(side * half, half), half)
        return pltpu.make_async_copy(
            out_v.at[which, :, ch], res_out.at[:, ch, where, :], sem.at[which, ch]
        )

    for which, (mod, vi, base, side) in enumerate(sides):
        outer_products(a_v.at[which], g_r2[side], g)

        for ch in range(fin):
            picks = [idx[d, e * fin + ch] for d in range(4)]
            for t in range(half // TILE):
                rows = slice(t * TILE, (t + 1) * TILE)
                re, im = residual_tile(a_v.at[which], mod, vi, base + ch, picks, rows)
                out_v[which, 0, ch, rows, :] = re
                out_v[which, 1, ch, rows, :] = im
            moved(which, ch).start()
    gains_copy.wait()
    for which in range(2):
        for ch in range(fin):
            moved(which, ch).wait()


def body(n_row, n_col, vis, model, gains, channel_interval_index, antenna_usable_mask):
    dirs, _, chans, rows, cols = model.shape
    half = rows // 2
    fin = chans // 2
    n_dir = 2 * dirs
    hbm = pl.BlockSpec(memory_space=pltpu.HBM)
    vmem = pl.BlockSpec(memory_space=pltpu.VMEM)
    smem = pl.BlockSpec(memory_space=pltpu.SMEM)
    dma = pltpu.SemaphoreType.DMA
    held = (
        pltpu.VMEM((n_dir, 2, chans, half, cols), BF16),
        pltpu.VMEM((2, chans, half, cols), BF16),
        pltpu.VMEM((n_dir, 2, fin, half, cols), BF16),
        pltpu.VMEM((2, fin, half, cols), BF16),
        pltpu.VMEM((2, 16, half), F32),
        pltpu.VMEM((16, cols), F32),
        pltpu.SMEM((n_dir, chans), jnp.int32),
    )
    spaces = (vmem,) * 6 + (smem,)
    args = [
        pltpu.with_memory_space_constraint(x, pltpu.HBM)
        for x in (vis, model, gains, antenna_usable_mask, channel_interval_index)
    ]
    state = pl.pallas_call(
        functools.partial(kernel, n_row, n_col),
        out_shape=held,
        in_specs=[hbm] * 5,
        out_specs=spaces,
        scratch_shapes=[
            pltpu.VMEM((chans, half, cols), BF16),
            pltpu.VMEM((4, 2 * half, cols), BF16),
            pltpu.VMEM((8, half, 2 * cols), F32),
            pltpu.VMEM((chans + 1, n_dir, 2 * half, cols), BF16),
            pltpu.VMEM((chans, half), jnp.int32),
            pltpu.VMEM((chans, cols), jnp.int32),
            pltpu.SMEM((n_dir, chans), jnp.int32),
            pltpu.SMEM((2, n_dir), jnp.int32),
            pltpu.VMEM((2,) + gains.shape, F32),
            pltpu.VMEM((2,) + gains.shape, F32),
            pltpu.VMEM((16, half), F32),
            pltpu.VMEM((ITERS, n_row, 16, cols), F32),
            pltpu.VMEM((ITERS, n_row, 8, cols), F32),
            pltpu.VMEM((ITERS, n_col, 16, half), F32),
            pltpu.VMEM((ITERS, n_col, 8, half), F32),
            pltpu.VMEM((1, n_row, 16, cols), BF16),
            pltpu.VMEM((1, n_row, 16, half), BF16),
            pltpu.VMEM((1, n_col, 16, half), BF16),
            pltpu.VMEM((ITERS, 2, 24, cols), F32),
            pltpu.SemaphoreType.REGULAR,
            dma((8,)),
            dma((chans + 1,)),
            dma((chans + 1,)),
            dma,
            dma,
            dma((n_col,)),
            dma((2,)),
            dma((ITERS, n_row)),
            dma((ITERS, n_row)),
            dma((ITERS, n_row)),
            dma((ITERS, n_row)),
            dma((ITERS, n_col)),
            dma((ITERS, n_col)),
            dma((ITERS, n_col)),
            dma((ITERS, n_col)),
            dma((ITERS,)),
            dma((ITERS, 2)),
            dma,
            dma((2,)),
        ],
        compiler_params=pltpu.CompilerParams(
            collective_id=0, has_side_effects=True, vmem_limit_bytes=24 * 2**20
        ),
    )(*args)
    return pl.pallas_call(
        finish_kernel,
        out_shape=(
            pltpu.HBM(gains.shape, F32),
            pltpu.HBM((2, fin, rows, cols), F32),
        ),
        in_specs=spaces,
        out_specs=(hbm, hbm),
        scratch_shapes=[
            pltpu.VMEM((2, 8, half, 2 * cols), F32),
            pltpu.VMEM((2, 2, fin, half, cols), F32),
            pltpu.VMEM(gains.shape, F32),
            dma((2, fin)),
            dma,
        ],
        compiler_params=pltpu.CompilerParams(vmem_limit_bytes=16 * 2**20),
    )(*state)


def solution(mesh):
    placed = (
        P(None, None, "row", "col"),
        P("dir", None, None, "row", "col"),
        P(None, "dir", None, "col"),
        P(),
        P(),
    )
    return jax.shard_map(
        functools.partial(body, mesh.shape["row"], mesh.shape["col"]),
        mesh=mesh,
        in_specs=placed,
        out_specs=(P(None, "dir", None, "col"), P(None, "dir", "row", "col")),
        check_vma=False,
    )
```

```python
import functools

import jax
import jax.numpy as jnp
from jax import lax
from jax.experimental import pallas as pl
from jax.experimental.pallas import tpu as pltpu
from jax.sharding import PartitionSpec as P

ITERS = 2
MESH = pl.DeviceIdType.MESH
F32, BF16 = jnp.float32, jnp.bfloat16
TILE = 16


def rows_like(shape):
    return lax.broadcasted_iota(jnp.int32, shape, 0)


def turned(g):
    count = g.shape[0] // 8
    out = []
    for k in range(count):
        out += [-g[8 * k + 4 : 8 * k + 8], g[8 * k : 8 * k + 4]]
    return jnp.concatenate(out, axis=0)


def halves(x):
    high = x.astype(BF16)
    return high, (x - high.astype(F32)).astype(BF16)


def outer_products(a_ref, g_rows, g_cols):
    count, width = g_rows.shape[1], g_cols.shape[1]
    right_hi, right_lo = halves(jnp.concatenate([g_cols, turned(g_cols)], axis=1))
    right = jnp.concatenate([right_hi, right_lo, right_hi], axis=0)
    left_hi, left_lo = halves(g_rows)
    left = jnp.concatenate([left_hi, left_hi, left_lo], axis=0).astype(F32).T
    lane = lax.broadcasted_iota(jnp.int32, left.shape, 1) % 16
    across = g_rows.T
    for d in range(4):
        keep = (lane == d) | (lane == 4 + d)
        a_ref[d] = jnp.dot(
            jnp.where(keep, left, 0.0).astype(BF16), right, preferred_element_type=F32
        )
        q_re, q_im = g_cols[8 + d : 9 + d, :], g_cols[12 + d : 13 + d, :]
        for t in range(count // 8):
            rows = slice(t * 8, (t + 1) * 8)
            p_re, p_im = across[rows, 8 + d : 9 + d], across[rows, 12 + d : 13 + d]
            a_ref[4 + d, rows, 0:width] = p_re * q_re + p_im * q_im
            a_ref[4 + d, rows, width : 2 * width] = p_im * q_re - p_re * q_im


def residual_tile(a, mod, vi, ch, picks, rows, vi_ch=None):
    vi_ch = ch if vi_ch is None else vi_ch
    re = vi[0, vi_ch, rows, :].astype(F32)
    im = vi[1, vi_ch, rows, :].astype(F32)
    width = re.shape[1]
    for d in range(4):
        at = picks[d] * 4 + d
        a_re = a[at, rows, 0:width]
        a_im = a[at, rows, width : 2 * width]
        m_re = mod[d, 0, ch, rows, :].astype(F32)
        m_im = mod[d, 1, ch, rows, :].astype(F32)
        re = re - a_re * m_re + a_im * m_im
        im = im - a_re * m_im - a_im * m_re
    return re, im


def kernel(
    n_row, n_col,
    vis, model, gains, mask, index,
    m_w, mf_w, v_w, g_r2, g_c, idx,
    m_v, v_v, mf_v, vf_v, w_v, d_v, a_v, t_v, fri_v, fci_v, prev, last,
    gin_c, gin_r, g_r, coln, cold, rown, rowd, colns, colds, rowns, colt,
    late, loc_sem, mod_s, mod_r, gs_s, gs_r, gr_s, gr_r,
    cn_s, cn_r, cd_s, cd_r, rn_s, rn_r, rd_s, rd_r, ct_s, ct_r, fin_s, fin_r,
):
    r, c, e = lax.axis_index("row"), lax.axis_index("col"), lax.axis_index("dir")
    other = 1 - e
    sib = (r, c, other)
    half = model.shape[3] // 2
    chans = model.shape[2]
    fin = chans // 2
    quad = n_col // 2

    def row_peer(k):
        return lax.rem(r + k, n_row), c, e

    def col_peer(k):
        return r, lax.rem(c + k, n_col), e

    row_list = sorted(range(1, n_row), key=lambda k: (k % 2 == 0, abs(k - n_row // 2)))
    col_list = sorted(range(1, n_col), key=lambda k: abs(k - n_col // 2))

    flip_r = r + 1 - 2 * lax.rem(r, 2)
    flip_c = c + 1 - 2 * lax.rem(c, 2)
    near = r == c
    cross = r == flip_c
    same = lax.div(r, quad) == lax.div(c, quad)
    source_row = jnp.where(same, r, flip_r)
    near_to = [
        (r, lax.div(c, quad) * quad + lax.rem(c + k, quad), x)
        for k in range(1, quad) for x in range(2)
    ]
    cross_to = [
        (c, (1 - lax.div(c, quad)) * quad + k, x) for k in range(quad) for x in range(2)
    ]

    barrier = pltpu.get_barrier_semaphore()

    @pl.when(jnp.logical_not(near))
    def _():
        for x in range(2):
            pl.semaphore_signal(
                barrier, inc=1, device_id=(source_row, r, x), device_id_type=MESH
            )

    holder = near | cross
    partners = []
    for k in col_list:
        to = col_peer(k)
        partners.append((to, (to[1] == r) | (to[1] == flip_r)))
    for k in row_list:
        to = row_peer(k)
        partners.append((to, (to[0] == c) | (to[0] == flip_c)))
    for to, holds in partners:

        @pl.when(holder | jnp.logical_not(holds))
        def _(to=to):
            pl.semaphore_signal(barrier, inc=1, device_id=to, device_id_type=MESH)

    pl.semaphore_signal(barrier, inc=1, device_id=sib, device_id_type=MESH)

    mine = pl.ds(pl.multiple_of(e * half, half), half)
    theirs = pl.ds(pl.multiple_of(other * half, half), half)
    my_ch = pl.ds(e * fin, fin)
    their_ch = pl.ds(other * fin, fin)
    block_r = pl.ds(pl.multiple_of(r * 2 * half + e * half, half), half)
    block_c = pl.ds(pl.multiple_of(c * 2 * half, 2 * half), 2 * half)
    own_dirs = pl.ds(2 * e, 2)
    local = [
        (gains, gin_c.at[e]),
        (index, idx),
        (mask.at[:, block_r], fri_v),
        (mask.at[:, block_c], fci_v),
        (model.at[:, :, :, mine, :], m_v.at[own_dirs]),
        (vis.at[:, :, mine, :], v_v),
        (vis.at[:, my_ch, theirs, :], vf_v),
        (model.at[:, :, my_ch, theirs, :], mf_v.at[own_dirs]),
    ]
    local = [pltpu.make_async_copy(s, d, loc_sem.at[i]) for i, (s, d) in enumerate(local)]
    for cp in local:
        cp.start()

    def remote(src, dst, send, recv, device):
        return pltpu.make_async_remote_copy(
            src_ref=src, dst_ref=dst, send_sem=send, recv_sem=recv,
            device_id=device, device_id_type=MESH,
        )

    local[0].wait()
    n_near, n_cross = len(near_to), len(cross_to)
    pl.semaphore_wait(
        barrier,
        jnp.where(holder, 2, len(partners)) + 1
        + jnp.where(near, n_near, 0) + jnp.where(cross, n_cross, 0),
    )

    def gains_to(devices):
        return [
            remote(gin_c.at[e], gin_r.at[e], gr_s.at[i], gr_r.at[e], to)
            for i, to in enumerate(devices)
        ]

    @pl.when(near)
    def _():
        for cp in gains_to(near_to):
            cp.start()

    @pl.when(cross)
    def _():
        for cp in gains_to(cross_to):
            cp.start()

    gains_sib = remote(gin_c.at[e], gin_c.at[e], gs_s, gs_r, sib)
    gains_sib.start()

    def chunk(ch, dirs):
        return remote(
            model.at[:, :, ch, theirs, :], m_v.at[dirs, :, ch], mod_s.at[ch], mod_r.at[ch], sib
        )

    model_a = [chunk(ch, own_dirs) for ch in range(chans)]
    model_b = remote(
        model.at[:, :, their_ch, mine, :], mf_v.at[own_dirs],
        mod_s.at[chans], mod_r.at[chans], sib,
    )
    for cp in model_a:
        cp.start()
    model_b.start()

    for to, holds in partners:

        @pl.when(jnp.logical_not(holder) & holds)
        def _(to=to):
            pl.semaphore_signal(late, inc=1, device_id=to, device_id_type=MESH)

    for cp in local[1:4]:
        cp.wait()
    for d in range(4):
        ends = [jnp.int32(chans), jnp.int32(chans)]
        for ch in range(chans):
            second = idx[d, ch] == 1
            prev[d, ch] = jnp.where(second, ends[1], ends[0])
            ends = [jnp.where(second, ends[0], ch), jnp.where(second, ch, ends[1])]
        for k in range(2):
            last[k, d] = ends[k]
    t_v[chans] = jnp.zeros(t_v.shape[1:], BF16)
    shape = (half, 2 * half)
    p_at = r * 2 * half + e * half + rows_like(shape)
    q_at = c * 2 * half + lax.broadcasted_iota(jnp.int32, shape, 1)
    apart = p_at != q_at
    f_r = fri_v[...].astype(F32)
    f_c = fci_v[...].astype(F32).astype(BF16)
    for ch in range(chans):
        one = jnp.where(rows_like(f_r.shape) == ch, f_r, 0.0).astype(BF16)
        both = lax.dot_general(
            one, f_c, (((0,), (0,)), ((), ())), preferred_element_type=F32
        )
        w_v[ch] = jnp.where(apart, both, 0.0).astype(BF16)

    def squares(core, l):
        d = 2 * core + l

        def tile(t, _):
            at = pl.multiple_of(t * TILE, TILE)
            rows = pl.ds(at, TILE)
            total = [jnp.zeros((TILE, 2 * half), F32)] * 2
            for ch in range(chans):
                re = m_v[d, 0, ch, rows, :].astype(F32)
                im = m_v[d, 1, ch, rows, :].astype(F32)
                sq = (re * re + im * im) * w_v[ch, rows, :].astype(F32)
                second = idx[d, ch].astype(F32)
                part = sq * second
                total = [total[0] + sq, total[1] + part]
            out = pl.ds(pl.multiple_of(l * half + at, TILE), TILE)
            d_v[core, out, :] = (total[0] - total[1]).astype(BF16)
            d_v[2 + core, out, :] = total[1].astype(BF16)
            return 0

        lax.fori_loop(0, half // TILE, tile, 0)

    local[4].wait()
    for l in range(2):
        squares(e, l)

    gains_sib.wait_recv()
    for s in range(2):
        for x in range(2):
            for l in range(2):
                for k in range(2):
                    at = k * 8 + x * 4 + s * 2 + l
                    g_c[at : at + 1, :] = gin_c[s, x, l, k : k + 1, :]

    @pl.when(near)
    def _():
        gin_r[...] = gin_c[...]

    @pl.when(jnp.logical_not(near))
    def _():
        for s in range(2):
            remote(gin_c.at[s], gin_r.at[s], gr_s.at[0], gr_r.at[s], sib).wait_recv()

    lanes = pl.ds(pl.multiple_of(e * half, half), half)
    for s in range(2):
        for x in range(2):
            for l in range(2):
                for k in range(2):
                    at = k * 8 + x * 4 + s * 2 + l
                    g_r[at : at + 1, :] = gin_r[s, x, l, k : k + 1, lanes]
    local[5].wait()

    def widen(pairs):
        for dst, src in pairs:
            for t in range(half // (2 * TILE)):
                rows = slice(t * 2 * TILE, (t + 1) * 2 * TILE)
                dst[rows, :] = src[rows, :].astype(F32)

    def widen_model(ch, _):
        widen([(m_w.at[d, x, ch], m_v.at[d, x, ch]) for d in range(4) for x in range(2)])
        return 0

    def widen_rest(ch, _):
        widen([(mf_w.at[d, x, ch], mf_v.at[d, x, ch]) for d in range(4) for x in range(2)])
        widen([(v_w.at[0, x, ch], v_v.at[x, e * fin + ch]) for x in range(2)])
        widen([(v_w.at[1, x, ch], vf_v.at[x, ch]) for x in range(2)])
        return 0

    def sweep(step, error):
        gr, gc = g_r[...], g_c[...]
        short = step == 0
        at16 = rows_like((16, 2 * half))
        at8 = rows_like((8, half))
        copies = []

        def send(buf, at, sems, ks, peer):
            for k in ks:
                cp = remote(
                    buf.at[step, at], buf.at[step, at], sems[0].at[step, k],
                    sems[1].at[step, at], peer(k),
                )
                cp.start()
                copies.append(cp)

        def gathered(buf, sems, at, count, ks, peer):
            for k in ks:
                src = lax.rem(at + k, count)
                remote(
                    buf.at[step, src], buf.at[step, src], sems[0].at[step, k],
                    sems[1].at[step, src], peer(k),
                ).wait_recv()
            total = buf[step, 0].astype(F32)
            for i in range(1, count):
                total = total + buf[step, i].astype(F32)
            return total

        def across(g, part):
            return lax.dot_general(g, part, (((1,), (1,)), ((), ())), preferred_element_type=F32)

        def squared(g):
            return jnp.concatenate(
                [g[8 * k : 8 * k + 4] ** 2 + g[8 * k + 4 : 8 * k + 8] ** 2 for k in range(2)],
                axis=0,
            )

        def denominators():
            s_r = squared(gr)
            s_c = squared(gc).astype(BF16)
            den_c = jnp.zeros((8, 2 * half), F32)
            den_r = jnp.zeros((8, half), F32)
            for k in range(2):
                for pair in range(2):
                    first = k * 4 + 2 * pair
                    left = jnp.concatenate(
                        [jnp.where(at8 == first + i, s_r, 0.0) for i in range(2)], axis=1
                    ).astype(BF16)
                    part = d_v[k * 2 + pair]
                    den_c += jnp.dot(left, part, preferred_element_type=F32)
                    got = across(s_c, part)
                    for i in range(2):
                        den_r = jnp.where(
                            at8 == first + i, got[:, i * half : (i + 1) * half], den_r
                        )
            rowd[step, c] = den_r
            send(rowd, c, (rd_s, rd_r), col_list, col_peer)
            if short:
                den_16 = den_c.astype(BF16)
                colds[step, r] = jnp.concatenate([den_16[:, :half], den_16[:, half:]], axis=0)
                send(colds, r, (cd_s, cd_r), row_list, row_peer)
                return den_c - den_16.astype(F32)
            cold[step, r] = den_c
            send(cold, r, (cd_s, cd_r), row_list, row_peer)
            return None

        def channel(ch, _):
            if step == 0:
                chunk(ch, pl.ds(2 * other, 2)).wait_recv()
            picks = [idx[d, ch] for d in range(4)]
            before = [prev[d, ch] for d in range(4)]
            for t in range(half // TILE):
                rows = slice(t * TILE, (t + 1) * TILE)
                below = slice(half + t * TILE, half + (t + 1) * TILE)
                re, im = residual_tile(a_v, m_v if short else m_w, v_v, ch, picks, rows)
                w = w_v[ch, rows, :]
                re = re.astype(BF16) * w
                im = im.astype(BF16) * w
                for d in range(4):
                    m_re = m_v[d, 0, ch, rows, :]
                    m_im = m_v[d, 1, ch, rows, :]
                    old_re = t_v[before[d], d, rows, :]
                    old_im = t_v[before[d], d, below, :]
                    t_v[ch, d, rows, :] = old_re + (re * m_re + im * m_im)
                    t_v[ch, d, below, :] = old_im + (re * m_im - im * m_re)
            return 0

        def all_parts(product):
            out = jnp.zeros((16, 2 * half), F32)
            for k in range(2):
                for d in range(4):
                    keep = (at16 == 8 * k + d) | (at16 == 8 * k + 4 + d)
                    out = jnp.where(keep, product(t_v[last[k, d], d]), out)
            return out

        if step > 0:
            denominators()
        outer_products(a_v, gr, gc)
        lax.fori_loop(0, chans, channel, 0)
        if step == 0:

            @pl.when(holder)
            def _():
                pl.semaphore_wait(late, len(partners) - 2)

        x_row = gc.astype(BF16)
        x_col = jnp.concatenate([gr, turned(gr)], axis=1).astype(BF16)
        o_row = all_parts(lambda part: across(x_row, part))
        o_row = o_row[:, :half] - turned(o_row[:, half:])
        if short:
            rowns[step, c] = o_row.astype(BF16)
            send(rowns, c, (rn_s, rn_r), col_list, col_peer)
        else:
            rown[step, c] = o_row + error[0]
            send(rown, c, (rn_s, rn_r), col_list, col_peer)
        o_col = all_parts(lambda part: jnp.dot(x_col, part, preferred_element_type=F32))
        if short:
            colns[step, r] = o_col.astype(BF16)
            send(colns, r, (cn_s, cn_r), row_list, row_peer)
            for l in range(2):
                squares(other, l)
            lost_den = denominators()
            lax.fori_loop(0, chans, widen_model, 0)
        else:
            coln[step, r] = o_col + error[1]
            send(coln, r, (cn_s, cn_r), row_list, row_peer)
            for cp in local[6:]:
                cp.wait()
            remote(
                model.at[:, :, their_ch, mine, :], mf_v.at[pl.ds(2 * other, 2)],
                mod_s.at[chans], mod_r.at[chans], sib,
            ).wait_recv()
            lax.fori_loop(0, fin, widen_rest, 0)

        def refresh(total, den):
            den = den + 1.0
            den = jnp.concatenate([den[0:4], den[0:4], den[4:8], den[4:8]], axis=0)
            return 0.5 * total / den

        total = gathered(colns if short else coln, (cn_s, cn_r), r, n_row, row_list, row_peer)
        total_den = gathered(colds if short else cold, (cd_s, cd_r), r, n_row, row_list, row_peer)
        if short:
            total_den = jnp.concatenate([total_den[0:8], total_den[8:16]], axis=1)
        colt[step, e] = jnp.concatenate([total, total_den], axis=0)
        both = remote(
            colt.at[step, e], colt.at[step, e], ct_s.at[step], ct_r.at[step, e], sib
        )
        both.start()
        copies.append(both)
        total = gathered(rowns if short else rown, (rn_s, rn_r), c, n_col, col_list, col_peer)
        total_den = gathered(rowd, (rd_s, rd_r), c, n_col, col_list, col_peer)
        change_r = refresh(total, total_den)
        g_r[...] = gr + change_r
        if step == ITERS - 1:
            g_r2[e] = g_r[...]
            rows_sib = remote(g_r2.at[e], g_r2.at[e], fin_s, fin_r.at[e], sib)
            rows_sib.start()
            copies.append(rows_sib)
        remote(
            colt.at[step, other], colt.at[step, other], ct_s.at[step], ct_r.at[step, other], sib
        ).wait_recv()
        total = colt[step, 0] + colt[step, 1]
        change_c = refresh(total[0:16], total[16:24])
        g_c[...] = gc + change_c
        if short:
            lost_r = o_row - rowns[step, c].astype(F32)
            lost_c = o_col - colns[step, r].astype(F32)
            lost_den = jnp.concatenate(
                [lost_den[0:4], lost_den[0:4], lost_den[4:8], lost_den[4:8]], axis=0
            )
            error = (0.5 * lost_r, 0.5 * lost_c - change_c * lost_den)
        return copies, error

    copies, error = [], None
    for step in range(ITERS):
        started, error = sweep(step, error)
        copies += started

    remote(g_r2.at[other], g_r2.at[other], fin_s, fin_r.at[other], sib).wait_recv()

    for cp in model_a + [model_b, gains_sib]:
        cp.wait_send()

    @pl.when(near)
    def _():
        for cp in gains_to(near_to):
            cp.wait_send()

    @pl.when(cross)
    def _():
        for cp in gains_to(cross_to):
            cp.wait_send()

    for cp in copies:
        cp.wait_send()


def finish_kernel(m_w, mf_w, v_w, g_r2, g_c, idx, gains_out, res_out, a_v, out_v, g_v, sem, g_sem):
    e = lax.axis_index("dir")
    half = m_w.shape[3]
    fin = mf_w.shape[2]
    g = g_c[...]
    for x in range(2):
        for l in range(2):
            for k in range(2):
                at = k * 8 + x * 4 + l
                g_v[x, l, k : k + 1, :] = jnp.where(e == 0, g[at : at + 1], g[at + 2 : at + 3])
    gains_copy = pltpu.make_async_copy(g_v, gains_out, g_sem)
    gains_copy.start()
    sides = (
        (m_w, v_w.at[0], e * fin, e),
        (mf_w, v_w.at[1], 0, 1 - e),
    )

    def moved(which, ch):
        side = sides[which][3]
        where = pl.ds(pl.multiple_of(side * half, half), half)
        return pltpu.make_async_copy(
            out_v.at[which, :, ch], res_out.at[:, ch, where, :], sem.at[which, ch]
        )

    for which, (mod, vi, base, side) in enumerate(sides):
        outer_products(a_v.at[which], g_r2[side], g)

        for ch in range(fin):
            picks = [idx[d, e * fin + ch] for d in range(4)]
            for t in range(half // TILE):
                rows = slice(t * TILE, (t + 1) * TILE)
                re, im = residual_tile(a_v.at[which], mod, vi, base + ch, picks, rows, ch)
                out_v[which, 0, ch, rows, :] = re
                out_v[which, 1, ch, rows, :] = im
            moved(which, ch).start()
    gains_copy.wait()
    for which in range(2):
        for ch in range(fin):
            moved(which, ch).wait()


def body(n_row, n_col, vis, model, gains, channel_interval_index, antenna_usable_mask):
    dirs, _, chans, rows, cols = model.shape
    half = rows // 2
    fin = chans // 2
    n_dir = 2 * dirs
    hbm = pl.BlockSpec(memory_space=pltpu.HBM)
    vmem = pl.BlockSpec(memory_space=pltpu.VMEM)
    smem = pl.BlockSpec(memory_space=pltpu.SMEM)
    dma = pltpu.SemaphoreType.DMA
    held = (
        pltpu.VMEM((n_dir, 2, chans, half, cols), F32),
        pltpu.VMEM((n_dir, 2, fin, half, cols), F32),
        pltpu.VMEM((2, 2, fin, half, cols), F32),
        pltpu.VMEM((2, 16, half), F32),
        pltpu.VMEM((16, cols), F32),
        pltpu.SMEM((n_dir, chans), jnp.int32),
    )
    spaces = (vmem,) * 5 + (smem,)
    args = [
        pltpu.with_memory_space_constraint(x, pltpu.HBM)
        for x in (vis, model, gains, antenna_usable_mask, channel_interval_index)
    ]
    state = pl.pallas_call(
        functools.partial(kernel, n_row, n_col),
        out_shape=held,
        in_specs=[hbm] * 5,
        out_specs=spaces,
        scratch_shapes=[
            pltpu.VMEM((n_dir, 2, chans, half, cols), BF16),
            pltpu.VMEM((2, chans, half, cols), BF16),
            pltpu.VMEM((n_dir, 2, fin, half, cols), BF16),
            pltpu.VMEM((2, fin, half, cols), BF16),
            pltpu.VMEM((chans, half, cols), BF16),
            pltpu.VMEM((4, 2 * half, cols), BF16),
            pltpu.VMEM((8, half, 2 * cols), F32),
            pltpu.VMEM((chans + 1, n_dir, 2 * half, cols), BF16),
            pltpu.VMEM((chans, half), jnp.int32),
            pltpu.VMEM((chans, cols), jnp.int32),
            pltpu.SMEM((n_dir, chans), jnp.int32),
            pltpu.SMEM((2, n_dir), jnp.int32),
            pltpu.VMEM((2,) + gains.shape, F32),
            pltpu.VMEM((2,) + gains.shape, F32),
            pltpu.VMEM((16, half), F32),
            pltpu.VMEM((ITERS, n_row, 16, cols), F32),
            pltpu.VMEM((ITERS, n_row, 8, cols), F32),
            pltpu.VMEM((ITERS, n_col, 16, half), F32),
            pltpu.VMEM((ITERS, n_col, 8, half), F32),
            pltpu.VMEM((1, n_row, 16, cols), BF16),
            pltpu.VMEM((1, n_row, 16, half), BF16),
            pltpu.VMEM((1, n_col, 16, half), BF16),
            pltpu.VMEM((ITERS, 2, 24, cols), F32),
            pltpu.SemaphoreType.REGULAR,
            dma((8,)),
            dma((chans + 1,)),
            dma((chans + 1,)),
            dma,
            dma,
            dma((n_col,)),
            dma((2,)),
            dma((ITERS, n_row)),
            dma((ITERS, n_row)),
            dma((ITERS, n_row)),
            dma((ITERS, n_row)),
            dma((ITERS, n_col)),
            dma((ITERS, n_col)),
            dma((ITERS, n_col)),
            dma((ITERS, n_col)),
            dma((ITERS,)),
            dma((ITERS, 2)),
            dma,
            dma((2,)),
        ],
        compiler_params=pltpu.CompilerParams(
            collective_id=0, has_side_effects=True, vmem_limit_bytes=28 * 2**20
        ),
    )(*args)
    return pl.pallas_call(
        finish_kernel,
        out_shape=(
            pltpu.HBM(gains.shape, F32),
            pltpu.HBM((2, fin, rows, cols), F32),
        ),
        in_specs=spaces,
        out_specs=(hbm, hbm),
        scratch_shapes=[
            pltpu.VMEM((2, 8, half, 2 * cols), F32),
            pltpu.VMEM((2, 2, fin, half, cols), F32),
            pltpu.VMEM(gains.shape, F32),
            dma((2, fin)),
            dma,
        ],
        compiler_params=pltpu.CompilerParams(vmem_limit_bytes=16 * 2**20),
    )(*state)


def solution(mesh):
    placed = (
        P(None, None, "row", "col"),
        P("dir", None, None, "row", "col"),
        P(None, "dir", None, "col"),
        P(),
        P(),
    )
    return jax.shard_map(
        functools.partial(body, mesh.shape["row"], mesh.shape["col"]),
        mesh=mesh,
        in_specs=placed,
        out_specs=(P(None, "dir", None, "col"), P(None, "dir", "row", "col")),
        check_vma=False,
    )
```

```python
import functools

import jax
import jax.numpy as jnp
from jax import lax
from jax.experimental import pallas as pl
from jax.experimental.pallas import tpu as pltpu
from jax.sharding import PartitionSpec as P

ITERS = 2
MESH = pl.DeviceIdType.MESH
F32, BF16 = jnp.float32, jnp.bfloat16
TILE = 16


def rows_like(shape):
    return lax.broadcasted_iota(jnp.int32, shape, 0)


def turned(g):
    count = g.shape[0] // 8
    out = []
    for k in range(count):
        out += [-g[8 * k + 4 : 8 * k + 8], g[8 * k : 8 * k + 4]]
    return jnp.concatenate(out, axis=0)


def halves(x):
    high = x.astype(BF16)
    return high, (x - high.astype(F32)).astype(BF16)


def outer_products(a_ref, g_rows, g_cols):
    count, width = g_rows.shape[1], g_cols.shape[1]
    right_hi, right_lo = halves(jnp.concatenate([g_cols, turned(g_cols)], axis=1))
    right = jnp.concatenate([right_hi, right_lo, right_hi], axis=0)
    left_hi, left_lo = halves(g_rows)
    left = jnp.concatenate([left_hi, left_hi, left_lo], axis=0).astype(F32).T
    lane = lax.broadcasted_iota(jnp.int32, left.shape, 1) % 16
    across = g_rows.T
    for d in range(4):
        keep = (lane == d) | (lane == 4 + d)
        a_ref[d] = jnp.dot(
            jnp.where(keep, left, 0.0).astype(BF16), right, preferred_element_type=F32
        )
        q_re, q_im = g_cols[8 + d : 9 + d, :], g_cols[12 + d : 13 + d, :]
        for t in range(count // 8):
            rows = slice(t * 8, (t + 1) * 8)
            p_re, p_im = across[rows, 8 + d : 9 + d], across[rows, 12 + d : 13 + d]
            a_ref[4 + d, rows, 0:width] = p_re * q_re + p_im * q_im
            a_ref[4 + d, rows, width : 2 * width] = p_im * q_re - p_re * q_im


def residual_tile(a, mod, vi, ch, picks, rows, vi_ch=None):
    vi_ch = ch if vi_ch is None else vi_ch
    re = vi[0, vi_ch, rows, :].astype(F32)
    im = vi[1, vi_ch, rows, :].astype(F32)
    width = re.shape[1]
    for d in range(4):
        at = picks[d] * 4 + d
        a_re = a[at, rows, 0:width]
        a_im = a[at, rows, width : 2 * width]
        m_re = mod[d, 0, ch, rows, :].astype(F32)
        m_im = mod[d, 1, ch, rows, :].astype(F32)
        re = re - a_re * m_re + a_im * m_im
        im = im - a_re * m_im - a_im * m_re
    return re, im


def kernel(
    n_row, n_col,
    vis, model, gains, mask, index,
    m_w, mf_w, v_w, g_r2, g_c, idx,
    m_v, v_v, mf_v, vf_v, mo_v, w_v, wo_v, d_v, d0_v, a_v, t_v, fri_v, fro_v, fci_v, prev, last,
    gin_c, gin_r, g_r, coln, cold, rown, rowd, colns, colds, rowns, rowds, dens, g_f, colt,
    late, loc_sem, mod_s, mod_r, gs_s, gs_r, gr_s, gr_r,
    cn_s, cn_r, cd_s, cd_r, rn_s, rn_r, rd_s, rd_r, ct_s, ct_r, ds_s, ds_r, fin_s, fin_r,
):
    r, c, e = lax.axis_index("row"), lax.axis_index("col"), lax.axis_index("dir")
    other = 1 - e
    sib = (r, c, other)
    half = model.shape[3] // 2
    chans = model.shape[2]
    fin = chans // 2
    quad = n_col // 2

    def row_peer(k):
        return lax.rem(r + k, n_row), c, e

    def col_peer(k):
        return r, lax.rem(c + k, n_col), e

    row_list = sorted(range(1, n_row), key=lambda k: (k % 2 == 0, abs(k - n_row // 2)))
    col_list = sorted(range(1, n_col), key=lambda k: abs(k - n_col // 2))

    flip_r = r + 1 - 2 * lax.rem(r, 2)
    flip_c = c + 1 - 2 * lax.rem(c, 2)
    near = r == c
    cross = r == flip_c
    same = lax.div(r, quad) == lax.div(c, quad)
    source_row = jnp.where(same, r, flip_r)
    near_to = [
        (r, lax.div(c, quad) * quad + lax.rem(c + k, quad), x)
        for k in range(1, quad) for x in range(2)
    ]
    cross_to = [
        (c, (1 - lax.div(c, quad)) * quad + k, x) for k in range(quad) for x in range(2)
    ]

    barrier = pltpu.get_barrier_semaphore()

    @pl.when(jnp.logical_not(near))
    def _():
        for x in range(2):
            pl.semaphore_signal(
                barrier, inc=1, device_id=(source_row, r, x), device_id_type=MESH
            )

    holder = near | cross
    partners = []
    for k in col_list:
        to = col_peer(k)
        partners.append((to, (to[1] == r) | (to[1] == flip_r)))
    for k in row_list:
        to = row_peer(k)
        partners.append((to, (to[0] == c) | (to[0] == flip_c)))
    for to, holds in partners:

        @pl.when(holder | jnp.logical_not(holds))
        def _(to=to):
            pl.semaphore_signal(barrier, inc=1, device_id=to, device_id_type=MESH)

    pl.semaphore_signal(barrier, inc=1, device_id=sib, device_id_type=MESH)

    mine = pl.ds(pl.multiple_of(e * half, half), half)
    theirs = pl.ds(pl.multiple_of(other * half, half), half)
    my_ch = pl.ds(e * fin, fin)
    their_ch = pl.ds(other * fin, fin)
    block_r = pl.ds(pl.multiple_of(r * 2 * half + e * half, half), half)
    block_o = pl.ds(pl.multiple_of(r * 2 * half + other * half, half), half)
    block_c = pl.ds(pl.multiple_of(c * 2 * half, 2 * half), 2 * half)
    own_dirs = pl.ds(2 * e, 2)
    local = [
        (gains, gin_c.at[e]),
        (index, idx),
        (mask.at[:, block_r], fri_v),
        (mask.at[:, block_c], fci_v),
        (model.at[:, :, :, mine, :], m_v.at[own_dirs]),
        (vis.at[:, :, mine, :], v_v),
        (vis.at[:, my_ch, theirs, :], vf_v),
        (model.at[:, :, my_ch, theirs, :], mf_v.at[own_dirs]),
        (mask.at[:, block_o], fro_v),
        (model.at[:, :, :, theirs, :], mo_v),
    ]
    local = [pltpu.make_async_copy(s, d, loc_sem.at[i]) for i, (s, d) in enumerate(local)]
    for cp in local:
        cp.start()

    def remote(src, dst, send, recv, device):
        return pltpu.make_async_remote_copy(
            src_ref=src, dst_ref=dst, send_sem=send, recv_sem=recv,
            device_id=device, device_id_type=MESH,
        )

    local[0].wait()
    n_near, n_cross = len(near_to), len(cross_to)
    pl.semaphore_wait(
        barrier,
        jnp.where(holder, 2, len(partners)) + 1
        + jnp.where(near, n_near, 0) + jnp.where(cross, n_cross, 0),
    )

    def gains_to(devices):
        return [
            remote(gin_c.at[e], gin_r.at[e], gr_s.at[i], gr_r.at[e], to)
            for i, to in enumerate(devices)
        ]

    @pl.when(near)
    def _():
        for cp in gains_to(near_to):
            cp.start()

    @pl.when(cross)
    def _():
        for cp in gains_to(cross_to):
            cp.start()

    gains_sib = remote(gin_c.at[e], gin_c.at[e], gs_s, gs_r, sib)
    gains_sib.start()

    def chunk(ch, dirs):
        return remote(
            model.at[:, :, ch, theirs, :], m_v.at[dirs, :, ch], mod_s.at[ch], mod_r.at[ch], sib
        )

    model_a = [chunk(ch, own_dirs) for ch in range(chans)]
    model_b = remote(
        model.at[:, :, their_ch, mine, :], mf_v.at[own_dirs],
        mod_s.at[chans], mod_r.at[chans], sib,
    )
    for cp in model_a:
        cp.start()
    model_b.start()

    for to, holds in partners:

        @pl.when(jnp.logical_not(holder) & holds)
        def _(to=to):
            pl.semaphore_signal(late, inc=1, device_id=to, device_id_type=MESH)

    for cp in local[1:4]:
        cp.wait()
    for d in range(4):
        ends = [jnp.int32(chans), jnp.int32(chans)]
        for ch in range(chans):
            second = idx[d, ch] == 1
            prev[d, ch] = jnp.where(second, ends[1], ends[0])
            ends = [jnp.where(second, ends[0], ch), jnp.where(second, ch, ends[1])]
        for k in range(2):
            last[k, d] = ends[k]
    t_v[chans] = jnp.zeros(t_v.shape[1:], BF16)
    local[8].wait()
    shape = (half, 2 * half)
    q_at = c * 2 * half + lax.broadcasted_iota(jnp.int32, shape, 1)
    f_c = fci_v[...].astype(F32).astype(BF16)
    for side, flags, out in ((e, fri_v, w_v), (other, fro_v, wo_v)):
        apart = r * 2 * half + side * half + rows_like(shape) != q_at
        f_r = flags[...].astype(F32)
        for ch in range(chans):
            one = jnp.where(rows_like(f_r.shape) == ch, f_r, 0.0).astype(BF16)
            both = lax.dot_general(
                one, f_c, (((0,), (0,)), ((), ())), preferred_element_type=F32
            )
            out[ch] = jnp.where(apart, both, 0.0).astype(BF16)

    def square_sums(mod, d, l, weights, store):
        def tile(t, _):
            at = pl.multiple_of(t * TILE, TILE)
            rows = pl.ds(at, TILE)
            total = [jnp.zeros((TILE, 2 * half), F32)] * 2
            for ch in range(chans):
                re = mod[l, 0, ch, rows, :].astype(F32)
                im = mod[l, 1, ch, rows, :].astype(F32)
                sq = (re * re + im * im) * weights[ch, rows, :].astype(F32)
                part = sq * idx[d, ch].astype(F32)
                total = [total[0] + sq, total[1] + part]
            store(at, (total[0] - total[1]).astype(BF16), total[1].astype(BF16))
            return 0

        lax.fori_loop(0, half // TILE, tile, 0)

    def squares(core, l, whole):
        def store(at, first, second):
            out = pl.ds(pl.multiple_of(l * half + at, TILE), TILE)
            d_v[core, out, :] = first
            d_v[2 + core, out, :] = second
            if whole:
                out = pl.ds(pl.multiple_of(e * half + at, TILE), TILE)
                d0_v[l, out, :] = first
                d0_v[2 + l, out, :] = second

        square_sums(m_v.at[pl.ds(2 * core, 2)], 2 * core + l, l, w_v, store)

    def squares_other_rows(l):
        def store(at, first, second):
            out = pl.ds(pl.multiple_of(other * half + at, TILE), TILE)
            d0_v[l, out, :] = first
            d0_v[2 + l, out, :] = second

        square_sums(mo_v, 2 * e + l, l, wo_v, store)

    local[4].wait()
    local[9].wait()
    for l in range(2):
        squares(e, l, True)
        squares_other_rows(l)

    gains_sib.wait_recv()
    for s in range(2):
        for x in range(2):
            for l in range(2):
                for k in range(2):
                    at = k * 8 + x * 4 + s * 2 + l
                    g_c[at : at + 1, :] = gin_c[s, x, l, k : k + 1, :]

    @pl.when(near)
    def _():
        gin_r[...] = gin_c[...]

    @pl.when(jnp.logical_not(near))
    def _():
        for s in range(2):
            remote(gin_c.at[s], gin_r.at[s], gr_s.at[0], gr_r.at[s], sib).wait_recv()

    lanes = pl.ds(pl.multiple_of(e * half, half), half)
    for s in range(2):
        for x in range(2):
            for l in range(2):
                for k in range(2):
                    at = k * 8 + x * 4 + s * 2 + l
                    g_r[at : at + 1, :] = gin_r[s, x, l, k : k + 1, lanes]
                    g_f[at : at + 1, :] = gin_r[s, x, l, k : k + 1, :]
    local[5].wait()

    def widen(pairs):
        for dst, src in pairs:
            for t in range(half // (2 * TILE)):
                rows = slice(t * 2 * TILE, (t + 1) * 2 * TILE)
                dst[rows, :] = src[rows, :].astype(F32)

    def widen_model(ch, _):
        widen([(m_w.at[d, x, ch], m_v.at[d, x, ch]) for d in range(4) for x in range(2)])
        return 0

    def widen_rest(ch, _):
        widen([(mf_w.at[d, x, ch], mf_v.at[d, x, ch]) for d in range(4) for x in range(2)])
        widen([(v_w.at[0, x, ch], v_v.at[x, e * fin + ch]) for x in range(2)])
        widen([(v_w.at[1, x, ch], vf_v.at[x, ch]) for x in range(2)])
        return 0

    def sweep(step, error):
        gr, gc = g_r[...], g_c[...]
        short = step == 0
        at16 = rows_like((16, 2 * half))
        at8 = rows_like((8, half))
        copies = []

        def to_all(buf, at, sems, ks, peer):
            made = [
                remote(
                    buf.at[step, at], buf.at[step, at], sems[0].at[step, k],
                    sems[1].at[step, at], peer(k),
                )
                for k in ks
            ]
            copies.extend(made)
            return made

        def send(*args):
            for cp in to_all(*args):
                cp.start()

        def gathered(buf, sems, at, count, ks, peer):
            for k in ks:
                src = lax.rem(at + k, count)
                remote(
                    buf.at[step, src], buf.at[step, src], sems[0].at[step, k],
                    sems[1].at[step, src], peer(k),
                ).wait_recv()
            total = buf[step, 0].astype(F32)
            for i in range(1, count):
                total = total + buf[step, i].astype(F32)
            return total

        def across(g, part):
            return lax.dot_general(g, part, (((1,), (1,)), ((), ())), preferred_element_type=F32)

        def squared(g):
            return jnp.concatenate(
                [g[8 * k : 8 * k + 4] ** 2 + g[8 * k + 4 : 8 * k + 8] ** 2 for k in range(2)],
                axis=0,
            )

        def denominators():
            s_r = squared(gr)
            s_c = squared(gc).astype(BF16)
            den_c = jnp.zeros((8, 2 * half), F32)
            den_r = jnp.zeros((8, half), F32)
            for k in range(2):
                for pair in range(2):
                    first = k * 4 + 2 * pair
                    left = jnp.concatenate(
                        [jnp.where(at8 == first + i, s_r, 0.0) for i in range(2)], axis=1
                    ).astype(BF16)
                    part = d_v[k * 2 + pair]
                    den_c += jnp.dot(left, part, preferred_element_type=F32)
                    got = across(s_c, part)
                    for i in range(2):
                        den_r = jnp.where(
                            at8 == first + i, got[:, i * half : (i + 1) * half], den_r
                        )
            rowd[step, c] = den_r
            send(rowd, c, (rd_s, rd_r), col_list, col_peer)
            cold[step, r] = den_c
            send(cold, r, (cd_s, cd_r), row_list, row_peer)

        def folded(x):
            return jnp.concatenate([x[0:4, :half], x[0:4, half:]], axis=0)

        def first_denominators():
            def own(sq):
                rows = [
                    jnp.where(e == 0, sq[4 * k : 4 * k + 2], sq[4 * k + 2 : 4 * k + 4])
                    for k in range(2)
                ]
                return jnp.concatenate(rows + [jnp.zeros_like(sq[0:4])], axis=0).astype(BF16)

            s_r, s_c = own(squared(g_f[...])), own(squared(gc))
            at = rows_like((8, 2 * half))
            den_c = jnp.zeros((8, 2 * half), F32)
            den_r = jnp.zeros((8, 2 * half), F32)
            for i in range(4):
                part = d0_v[i]
                got = jnp.dot(s_r, part, preferred_element_type=F32)
                den_c = jnp.where(at == i, got, den_c)
                den_r = jnp.where(at == i, across(s_c, part), den_r)
            rowds[step, c] = folded(den_r)
            colds[step, r] = folded(den_c)
            made = to_all(rowds, c, (rd_s, rd_r), col_list, col_peer)
            return made + to_all(colds, r, (cd_s, cd_r), row_list, row_peer)

        def channel(ch, _):
            if step == 0:
                chunk(ch, pl.ds(2 * other, 2)).wait_recv()
            picks = [idx[d, ch] for d in range(4)]
            before = [prev[d, ch] for d in range(4)]
            for t in range(half // TILE):
                rows = slice(t * TILE, (t + 1) * TILE)
                below = slice(half + t * TILE, half + (t + 1) * TILE)
                re, im = residual_tile(a_v, m_v if short else m_w, v_v, ch, picks, rows)
                w = w_v[ch, rows, :]
                re = re.astype(BF16) * w
                im = im.astype(BF16) * w
                for d in range(4):
                    m_re = m_v[d, 0, ch, rows, :]
                    m_im = m_v[d, 1, ch, rows, :]
                    old_re = t_v[before[d], d, rows, :]
                    old_im = t_v[before[d], d, below, :]
                    t_v[ch, d, rows, :] = old_re + (re * m_re + im * m_im)
                    t_v[ch, d, below, :] = old_im + (re * m_im - im * m_re)
            return 0

        def all_parts(product):
            out = jnp.zeros((16, 2 * half), F32)
            for k in range(2):
                for d in range(4):
                    keep = (at16 == 8 * k + d) | (at16 == 8 * k + 4 + d)
                    out = jnp.where(keep, product(t_v[last[k, d], d]), out)
            return out

        outer_products(a_v, gr, gc)
        if short:
            first = first_denominators()

            @pl.when(jnp.logical_not(holder))
            def _():
                for cp in first:
                    cp.start()

        else:
            denominators()
        lax.fori_loop(0, chans, channel, 0)
        if short:

            @pl.when(holder)
            def _():
                pl.semaphore_wait(late, len(partners) - 2)
                for cp in first:
                    cp.start()

        x_row = gc.astype(BF16)
        x_col = jnp.concatenate([gr, turned(gr)], axis=1).astype(BF16)
        o_row = all_parts(lambda part: across(x_row, part))
        o_row = o_row[:, :half] - turned(o_row[:, half:])
        if short:
            rowns[step, c] = o_row.astype(BF16)
            send(rowns, c, (rn_s, rn_r), col_list, col_peer)
        else:
            rown[step, c] = o_row + error[0]
            send(rown, c, (rn_s, rn_r), col_list, col_peer)
        o_col = all_parts(lambda part: jnp.dot(x_col, part, preferred_element_type=F32))
        if short:
            colns[step, r] = o_col.astype(BF16)
            send(colns, r, (cn_s, cn_r), row_list, row_peer)
            dens[e] = jnp.concatenate(
                [
                    gathered(colds, (cd_s, cd_r), r, n_row, row_list, row_peer),
                    gathered(rowds, (rd_s, rd_r), c, n_col, col_list, col_peer),
                ],
                axis=0,
            )
            dens_sib = remote(dens.at[e], dens.at[e], ds_s, ds_r.at[e], sib)
            dens_sib.start()
            copies.append(dens_sib)
            for l in range(2):
                squares(other, l, False)
            lax.fori_loop(0, chans, widen_model, 0)
        else:
            coln[step, r] = o_col + error[1]
            send(coln, r, (cn_s, cn_r), row_list, row_peer)
            for cp in local[6:8]:
                cp.wait()
            remote(
                model.at[:, :, their_ch, mine, :], mf_v.at[pl.ds(2 * other, 2)],
                mod_s.at[chans], mod_r.at[chans], sib,
            ).wait_recv()
            lax.fori_loop(0, fin, widen_rest, 0)

        def refresh(total, den):
            den = den + 1.0
            den = jnp.concatenate([den[0:4], den[0:4], den[4:8], den[4:8]], axis=0)
            return 0.5 * total / den

        total = gathered(colns if short else coln, (cn_s, cn_r), r, n_row, row_list, row_peer)
        if short:
            remote(dens.at[other], dens.at[other], ds_s, ds_r.at[other], sib).wait_recv()
            cores = []
            for i in range(2):
                part = dens[i]
                cores.append((
                    jnp.concatenate([part[0:4], part[4:8]], axis=1),
                    jnp.where(e == 0, part[8:12], part[12:16]),
                ))
            den_c, den_r = (
                jnp.concatenate([x[0:2], y[0:2], x[2:4], y[2:4]], axis=0)
                for x, y in zip(*cores)
            )
            total_den = jnp.zeros((8, 2 * half), F32)
        else:
            total_den = gathered(cold, (cd_s, cd_r), r, n_row, row_list, row_peer)
        colt[step, e] = jnp.concatenate([total, total_den], axis=0)
        both = remote(
            colt.at[step, e], colt.at[step, e], ct_s.at[step], ct_r.at[step, e], sib
        )
        both.start()
        copies.append(both)
        total = gathered(rowns if short else rown, (rn_s, rn_r), c, n_col, col_list, col_peer)
        if not short:
            den_r = gathered(rowd, (rd_s, rd_r), c, n_col, col_list, col_peer)
        change_r = refresh(total, den_r)
        g_r[...] = gr + change_r
        if step == ITERS - 1:
            g_r2[e] = g_r[...]
            rows_sib = remote(g_r2.at[e], g_r2.at[e], fin_s, fin_r.at[e], sib)
            rows_sib.start()
            copies.append(rows_sib)
        remote(
            colt.at[step, other], colt.at[step, other], ct_s.at[step], ct_r.at[step, other], sib
        ).wait_recv()
        total = colt[step, 0] + colt[step, 1]
        change_c = refresh(total[0:16], den_c if short else total[16:24])
        g_c[...] = gc + change_c
        if short:
            lost_r = o_row - rowns[step, c].astype(F32)
            lost_c = o_col - colns[step, r].astype(F32)
            error = (0.5 * lost_r, 0.5 * lost_c)
        return copies, error

    copies, error = [], None
    for step in range(ITERS):
        started, error = sweep(step, error)
        copies += started

    remote(g_r2.at[other], g_r2.at[other], fin_s, fin_r.at[other], sib).wait_recv()

    for cp in model_a + [model_b, gains_sib]:
        cp.wait_send()

    @pl.when(near)
    def _():
        for cp in gains_to(near_to):
            cp.wait_send()

    @pl.when(cross)
    def _():
        for cp in gains_to(cross_to):
            cp.wait_send()

    for cp in copies:
        cp.wait_send()


def finish_kernel(m_w, mf_w, v_w, g_r2, g_c, idx, gains_out, res_out, a_v, b_v, out_v, g_v, sem, g_sem):
    e = lax.axis_index("dir")
    half = m_w.shape[3]
    fin = mf_w.shape[2]
    g = g_c[...]
    for x in range(2):
        for l in range(2):
            for k in range(2):
                at = k * 8 + x * 4 + l
                g_v[x, l, k : k + 1, :] = jnp.where(e == 0, g[at : at + 1], g[at + 2 : at + 3])
    gains_copy = pltpu.make_async_copy(g_v, gains_out, g_sem)
    gains_copy.start()
    sides = (
        (m_w, v_w.at[0], e * fin, e),
        (mf_w, v_w.at[1], 0, 1 - e),
    )

    def moved(which, ch):
        side = sides[which][3]
        where = pl.ds(pl.multiple_of(side * half, half), half)
        return pltpu.make_async_copy(
            out_v.at[which, :, ch], res_out.at[:, ch, where, :], sem.at[which, ch]
        )

    products = (a_v, b_v)
    for which in range(2):
        outer_products(products[which], g_r2[sides[which][3]], g)
    for which, (mod, vi, base, side) in enumerate(sides):

        for ch in range(fin):
            picks = [idx[d, e * fin + ch] for d in range(4)]
            for t in range(half // TILE):
                rows = slice(t * TILE, (t + 1) * TILE)
                re, im = residual_tile(products[which], mod, vi, base + ch, picks, rows, ch)
                out_v[which, 0, ch, rows, :] = re
                out_v[which, 1, ch, rows, :] = im
            moved(which, ch).start()
    gains_copy.wait()
    for which in range(2):
        for ch in range(fin):
            moved(which, ch).wait()


def body(n_row, n_col, vis, model, gains, channel_interval_index, antenna_usable_mask):
    dirs, _, chans, rows, cols = model.shape
    half = rows // 2
    fin = chans // 2
    n_dir = 2 * dirs
    hbm = pl.BlockSpec(memory_space=pltpu.HBM)
    vmem = pl.BlockSpec(memory_space=pltpu.VMEM)
    smem = pl.BlockSpec(memory_space=pltpu.SMEM)
    dma = pltpu.SemaphoreType.DMA
    held = (
        pltpu.VMEM((n_dir, 2, chans, half, cols), F32),
        pltpu.VMEM((n_dir, 2, fin, half, cols), F32),
        pltpu.VMEM((2, 2, fin, half, cols), F32),
        pltpu.VMEM((2, 16, half), F32),
        pltpu.VMEM((16, cols), F32),
        pltpu.SMEM((n_dir, chans), jnp.int32),
    )
    spaces = (vmem,) * 5 + (smem,)
    args = [
        pltpu.with_memory_space_constraint(x, pltpu.HBM)
        for x in (vis, model, gains, antenna_usable_mask, channel_interval_index)
    ]
    state = pl.pallas_call(
        functools.partial(kernel, n_row, n_col),
        out_shape=held,
        in_specs=[hbm] * 5,
        out_specs=spaces,
        scratch_shapes=[
            pltpu.VMEM((n_dir, 2, chans, half, cols), BF16),
            pltpu.VMEM((2, chans, half, cols), BF16),
            pltpu.VMEM((n_dir, 2, fin, half, cols), BF16),
            pltpu.VMEM((2, fin, half, cols), BF16),
            pltpu.VMEM((2, 2, chans, half, cols), BF16),
            pltpu.VMEM((chans, half, cols), BF16),
            pltpu.VMEM((chans, half, cols), BF16),
            pltpu.VMEM((4, 2 * half, cols), BF16),
            pltpu.VMEM((4, 2 * half, cols), BF16),
            pltpu.VMEM((8, half, 2 * cols), F32),
            pltpu.VMEM((chans + 1, n_dir, 2 * half, cols), BF16),
            pltpu.VMEM((chans, half), jnp.int32),
            pltpu.VMEM((chans, half), jnp.int32),
            pltpu.VMEM((chans, cols), jnp.int32),
            pltpu.SMEM((n_dir, chans), jnp.int32),
            pltpu.SMEM((2, n_dir), jnp.int32),
            pltpu.VMEM((2,) + gains.shape, F32),
            pltpu.VMEM((2,) + gains.shape, F32),
            pltpu.VMEM((16, half), F32),
            pltpu.VMEM((ITERS, n_row, 16, cols), F32),
            pltpu.VMEM((ITERS, n_row, 8, cols), F32),
            pltpu.VMEM((ITERS, n_col, 16, half), F32),
            pltpu.VMEM((ITERS, n_col, 8, half), F32),
            pltpu.VMEM((1, n_row, 16, cols), BF16),
            pltpu.VMEM((1, n_row, 8, half), F32),
            pltpu.VMEM((1, n_col, 16, half), BF16),
            pltpu.VMEM((1, n_col, 8, half), F32),
            pltpu.VMEM((2, 16, half), F32),
            pltpu.VMEM((16, cols), F32),
            pltpu.VMEM((ITERS, 2, 24, cols), F32),
            pltpu.SemaphoreType.REGULAR,
            dma((10,)),
            dma((chans + 1,)),
            dma((chans + 1,)),
            dma,
            dma,
            dma((n_col,)),
            dma((2,)),
            dma((ITERS, n_row)),
            dma((ITERS, n_row)),
            dma((ITERS, n_row)),
            dma((ITERS, n_row)),
            dma((ITERS, n_col)),
            dma((ITERS, n_col)),
            dma((ITERS, n_col)),
            dma((ITERS, n_col)),
            dma((ITERS,)),
            dma((ITERS, 2)),
            dma,
            dma((2,)),
            dma,
            dma((2,)),
        ],
        compiler_params=pltpu.CompilerParams(
            collective_id=0, has_side_effects=True, vmem_limit_bytes=32 * 2**20
        ),
    )(*args)
    return pl.pallas_call(
        finish_kernel,
        out_shape=(
            pltpu.HBM(gains.shape, F32),
            pltpu.HBM((2, fin, rows, cols), F32),
        ),
        in_specs=spaces,
        out_specs=(hbm, hbm),
        scratch_shapes=[
            pltpu.VMEM((8, half, 2 * cols), F32),
            pltpu.VMEM((8, half, 2 * cols), F32),
            pltpu.VMEM((2, 2, fin, half, cols), F32),
            pltpu.VMEM(gains.shape, F32),
            dma((2, fin)),
            dma,
        ],
        compiler_params=pltpu.CompilerParams(vmem_limit_bytes=16 * 2**20),
    )(*state)


def solution(mesh):
    placed = (
        P(None, None, "row", "col"),
        P("dir", None, None, "row", "col"),
        P(None, "dir", None, "col"),
        P(),
        P(),
    )
    return jax.shard_map(
        functools.partial(body, mesh.shape["row"], mesh.shape["col"]),
        mesh=mesh,
        in_specs=placed,
        out_specs=(P(None, "dir", None, "col"), P(None, "dir", "row", "col")),
        check_vma=False,
    )
```

```python
import functools

import jax
import jax.numpy as jnp
from jax import lax
from jax.experimental import pallas as pl
from jax.experimental.pallas import tpu as pltpu
from jax.sharding import PartitionSpec as P

ITERS = 2
MESH = pl.DeviceIdType.MESH
F32, BF16 = jnp.float32, jnp.bfloat16
TILE = 16


def rows_like(shape):
    return lax.broadcasted_iota(jnp.int32, shape, 0)


def turned(g):
    count = g.shape[0] // 8
    out = []
    for k in range(count):
        out += [-g[8 * k + 4 : 8 * k + 8], g[8 * k : 8 * k + 4]]
    return jnp.concatenate(out, axis=0)


def halves(x):
    high = x.astype(BF16)
    return high, (x - high.astype(F32)).astype(BF16)


def outer_products(a_ref, g_rows, g_cols):
    count, width = g_rows.shape[1], g_cols.shape[1]
    right_hi, right_lo = halves(jnp.concatenate([g_cols, turned(g_cols)], axis=1))
    right = jnp.concatenate([right_hi, right_lo, right_hi], axis=0)
    left_hi, left_lo = halves(g_rows)
    left = jnp.concatenate([left_hi, left_hi, left_lo], axis=0).astype(F32).T
    lane = lax.broadcasted_iota(jnp.int32, left.shape, 1) % 16
    across = g_rows.T
    for d in range(4):
        keep = (lane == d) | (lane == 4 + d)
        a_ref[d] = jnp.dot(
            jnp.where(keep, left, 0.0).astype(BF16), right, preferred_element_type=F32
        )
        q_re, q_im = g_cols[8 + d : 9 + d, :], g_cols[12 + d : 13 + d, :]
        for t in range(count // 8):
            rows = slice(t * 8, (t + 1) * 8)
            p_re, p_im = across[rows, 8 + d : 9 + d], across[rows, 12 + d : 13 + d]
            a_ref[4 + d, rows, 0:width] = p_re * q_re + p_im * q_im
            a_ref[4 + d, rows, width : 2 * width] = p_im * q_re - p_re * q_im


def residual_tile(a, mod, vi, ch, picks, rows, vi_ch=None):
    vi_ch = ch if vi_ch is None else vi_ch
    re = vi[0, vi_ch, rows, :].astype(F32)
    im = vi[1, vi_ch, rows, :].astype(F32)
    width = re.shape[1]
    for d in range(4):
        at = picks[d] * 4 + d
        a_re = a[at, rows, 0:width]
        a_im = a[at, rows, width : 2 * width]
        m_re = mod[d, 0, ch, rows, :].astype(F32)
        m_im = mod[d, 1, ch, rows, :].astype(F32)
        re = re - a_re * m_re + a_im * m_im
        im = im - a_re * m_im - a_im * m_re
    return re, im


def kernel(
    n_row, n_col,
    vis, model, gains, mask, index,
    m_w, mf_w, v_w, g_r2, g_c, idx,
    m_v, v_v, mf_v, vf_v, mo_v, w_v, wo_v, d_v, d0_v, a_v, t_v, fri_v, fro_v, fci_v, prev, last,
    gin_c, gin_r, g_r, coln, cold, rown, rowd, colns, colds, rowns, rowds, dens, g_f, colt,
    late, loc_sem, mod_s, mod_r, gs_s, gs_r, gr_s, gr_r,
    cn_s, cn_r, cd_s, cd_r, rn_s, rn_r, rd_s, rd_r, ct_s, ct_r, ds_s, ds_r, fin_s, fin_r,
):
    r, c, e = lax.axis_index("row"), lax.axis_index("col"), lax.axis_index("dir")
    other = 1 - e
    sib = (r, c, other)
    half = model.shape[3] // 2
    chans = model.shape[2]
    fin = chans // 2
    quad = n_col // 2

    def row_peer(k):
        return lax.rem(r + k, n_row), c, e

    def col_peer(k):
        return r, lax.rem(c + k, n_col), e

    row_list = sorted(range(1, n_row), key=lambda k: (k % 2 == 0, abs(k - n_row // 2)))
    col_list = sorted(range(1, n_col), key=lambda k: abs(k - n_col // 2))

    flip_r = r + 1 - 2 * lax.rem(r, 2)
    flip_c = c + 1 - 2 * lax.rem(c, 2)
    near = r == c
    cross = r == flip_c
    same = lax.div(r, quad) == lax.div(c, quad)
    source_row = jnp.where(same, r, flip_r)
    near_to = [
        (r, lax.div(c, quad) * quad + lax.rem(c + k, quad), x)
        for k in range(1, quad) for x in range(2)
    ]
    cross_to = [
        (c, (1 - lax.div(c, quad)) * quad + k, x) for k in range(quad) for x in range(2)
    ]

    barrier = pltpu.get_barrier_semaphore()

    @pl.when(jnp.logical_not(near))
    def _():
        for x in range(2):
            pl.semaphore_signal(
                barrier, inc=1, device_id=(source_row, r, x), device_id_type=MESH
            )

    holder = near | cross
    partners = []
    for k in col_list:
        to = col_peer(k)
        partners.append((to, (to[1] == r) | (to[1] == flip_r)))
    for k in row_list:
        to = row_peer(k)
        partners.append((to, (to[0] == c) | (to[0] == flip_c)))
    for to, holds in partners:

        @pl.when(holder | jnp.logical_not(holds))
        def _(to=to):
            pl.semaphore_signal(barrier, inc=1, device_id=to, device_id_type=MESH)

    pl.semaphore_signal(barrier, inc=1, device_id=sib, device_id_type=MESH)

    mine = pl.ds(pl.multiple_of(e * half, half), half)
    theirs = pl.ds(pl.multiple_of(other * half, half), half)
    my_ch = pl.ds(e * fin, fin)
    their_ch = pl.ds(other * fin, fin)
    block_r = pl.ds(pl.multiple_of(r * 2 * half + e * half, half), half)
    block_o = pl.ds(pl.multiple_of(r * 2 * half + other * half, half), half)
    block_c = pl.ds(pl.multiple_of(c * 2 * half, 2 * half), 2 * half)
    own_dirs = pl.ds(2 * e, 2)
    local = [
        (gains, gin_c.at[e]),
        (index, idx),
        (mask.at[:, block_r], fri_v),
        (mask.at[:, block_c], fci_v),
        (model.at[:, :, :, mine, :], m_v.at[own_dirs]),
        (vis.at[:, :, mine, :], v_v),
        (vis.at[:, my_ch, theirs, :], vf_v),
        (model.at[:, :, my_ch, theirs, :], mf_v.at[own_dirs]),
        (mask.at[:, block_o], fro_v),
        (model.at[:, :, :, theirs, :], mo_v),
    ]
    local = [pltpu.make_async_copy(s, d, loc_sem.at[i]) for i, (s, d) in enumerate(local)]
    for cp in local:
        cp.start()

    def remote(src, dst, send, recv, device):
        return pltpu.make_async_remote_copy(
            src_ref=src, dst_ref=dst, send_sem=send, recv_sem=recv,
            device_id=device, device_id_type=MESH,
        )

    local[0].wait()
    n_near, n_cross = len(near_to), len(cross_to)
    pl.semaphore_wait(
        barrier,
        jnp.where(holder, 2, len(partners)) + 1
        + jnp.where(near, n_near, 0) + jnp.where(cross, n_cross, 0),
    )

    def gains_to(devices):
        return [
            remote(gin_c.at[e], gin_r.at[e], gr_s.at[i], gr_r.at[e], to)
            for i, to in enumerate(devices)
        ]

    @pl.when(near)
    def _():
        for cp in gains_to(near_to):
            cp.start()

    @pl.when(cross)
    def _():
        for cp in gains_to(cross_to):
            cp.start()

    gains_sib = remote(gin_c.at[e], gin_c.at[e], gs_s, gs_r, sib)
    gains_sib.start()

    def chunk(ch, dirs):
        return remote(
            model.at[:, :, ch, theirs, :], m_v.at[dirs, :, ch], mod_s.at[ch], mod_r.at[ch], sib
        )

    model_a = [chunk(ch, own_dirs) for ch in range(chans)]
    model_b = remote(
        model.at[:, :, their_ch, mine, :], mf_v.at[own_dirs],
        mod_s.at[chans], mod_r.at[chans], sib,
    )
    for cp in model_a:
        cp.start()
    model_b.start()

    for to, holds in partners:

        @pl.when(jnp.logical_not(holder) & holds)
        def _(to=to):
            pl.semaphore_signal(late, inc=1, device_id=to, device_id_type=MESH)

    for cp in local[1:4]:
        cp.wait()
    for d in range(4):
        ends = [jnp.int32(chans), jnp.int32(chans)]
        for ch in range(chans):
            second = idx[d, ch] == 1
            prev[d, ch] = jnp.where(second, ends[1], ends[0])
            ends = [jnp.where(second, ends[0], ch), jnp.where(second, ch, ends[1])]
        for k in range(2):
            last[k, d] = ends[k]
    t_v[chans] = jnp.zeros(t_v.shape[1:], BF16)
    local[8].wait()
    shape = (half, 2 * half)
    q_at = c * 2 * half + lax.broadcasted_iota(jnp.int32, shape, 1)
    f_c = fci_v[...].astype(F32).astype(BF16)
    for side, flags, out in ((e, fri_v, w_v), (other, fro_v, wo_v)):
        apart = r * 2 * half + side * half + rows_like(shape) != q_at
        f_r = flags[...].astype(F32)
        for ch in range(chans):
            one = jnp.where(rows_like(f_r.shape) == ch, f_r, 0.0).astype(BF16)
            both = lax.dot_general(
                one, f_c, (((0,), (0,)), ((), ())), preferred_element_type=F32
            )
            out[ch] = jnp.where(apart, both, 0.0).astype(BF16)

    def square_sums(mod, d, l, weights, store):
        def tile(t, _):
            at = pl.multiple_of(t * TILE, TILE)
            rows = pl.ds(at, TILE)
            total = [jnp.zeros((TILE, 2 * half), F32)] * 2
            for ch in range(chans):
                re = mod[l, 0, ch, rows, :].astype(F32)
                im = mod[l, 1, ch, rows, :].astype(F32)
                sq = (re * re + im * im) * weights[ch, rows, :].astype(F32)
                part = sq * idx[d, ch].astype(F32)
                total = [total[0] + sq, total[1] + part]
            store(at, (total[0] - total[1]).astype(BF16), total[1].astype(BF16))
            return 0

        lax.fori_loop(0, half // TILE, tile, 0)

    def squares(core, l, whole):
        def store(at, first, second):
            out = pl.ds(pl.multiple_of(l * half + at, TILE), TILE)
            d_v[core, out, :] = first
            d_v[2 + core, out, :] = second
            if whole:
                out = pl.ds(pl.multiple_of(e * half + at, TILE), TILE)
                d0_v[l, out, :] = first
                d0_v[2 + l, out, :] = second

        square_sums(m_v.at[pl.ds(2 * core, 2)], 2 * core + l, l, w_v, store)

    def squares_other_rows(l):
        def store(at, first, second):
            out = pl.ds(pl.multiple_of(other * half + at, TILE), TILE)
            d0_v[l, out, :] = first
            d0_v[2 + l, out, :] = second

        square_sums(mo_v, 2 * e + l, l, wo_v, store)

    local[4].wait()
    local[9].wait()
    for l in range(2):
        squares(e, l, True)
        squares_other_rows(l)

    gains_sib.wait_recv()
    for s in range(2):
        for x in range(2):
            for l in range(2):
                for k in range(2):
                    at = k * 8 + x * 4 + s * 2 + l
                    g_c[at : at + 1, :] = gin_c[s, x, l, k : k + 1, :]

    @pl.when(near)
    def _():
        gin_r[...] = gin_c[...]

    @pl.when(jnp.logical_not(near))
    def _():
        for s in range(2):
            remote(gin_c.at[s], gin_r.at[s], gr_s.at[0], gr_r.at[s], sib).wait_recv()

    lanes = pl.ds(pl.multiple_of(e * half, half), half)
    for s in range(2):
        for x in range(2):
            for l in range(2):
                for k in range(2):
                    at = k * 8 + x * 4 + s * 2 + l
                    g_r[at : at + 1, :] = gin_r[s, x, l, k : k + 1, lanes]
                    g_f[at : at + 1, :] = gin_r[s, x, l, k : k + 1, :]
    local[5].wait()

    def widen(pairs):
        for dst, src in pairs:
            for t in range(half // (2 * TILE)):
                rows = slice(t * 2 * TILE, (t + 1) * 2 * TILE)
                dst[rows, :] = src[rows, :].astype(F32)

    def widen_model(ch, _):
        widen([(m_w.at[d, x, ch], m_v.at[d, x, ch]) for d in range(4) for x in range(2)])
        return 0

    def widen_rest(ch, _):
        widen([(mf_w.at[d, x, ch], mf_v.at[d, x, ch]) for d in range(4) for x in range(2)])
        widen([(v_w.at[0, x, ch], v_v.at[x, e * fin + ch]) for x in range(2)])
        widen([(v_w.at[1, x, ch], vf_v.at[x, ch]) for x in range(2)])
        return 0

    def sweep(step, error):
        gr, gc = g_r[...], g_c[...]
        short = step == 0
        at16 = rows_like((16, 2 * half))
        at8 = rows_like((8, half))
        copies = []

        def to_all(buf, at, sems, ks, peer):
            made = [
                remote(
                    buf.at[step, at], buf.at[step, at], sems[0].at[step, k],
                    sems[1].at[step, at], peer(k),
                )
                for k in ks
            ]
            copies.extend(made)
            return made

        def send(*args):
            for cp in to_all(*args):
                cp.start()

        def gathered(buf, sems, at, count, ks, peer):
            for k in ks:
                src = lax.rem(at + k, count)
                remote(
                    buf.at[step, src], buf.at[step, src], sems[0].at[step, k],
                    sems[1].at[step, src], peer(k),
                ).wait_recv()
            total = buf[step, 0].astype(F32)
            for i in range(1, count):
                total = total + buf[step, i].astype(F32)
            return total

        def across(g, part):
            return lax.dot_general(g, part, (((1,), (1,)), ((), ())), preferred_element_type=F32)

        def squared(g):
            return jnp.concatenate(
                [g[8 * k : 8 * k + 4] ** 2 + g[8 * k + 4 : 8 * k + 8] ** 2 for k in range(2)],
                axis=0,
            )

        def denominators():
            s_r = squared(gr)
            s_c = squared(gc).astype(BF16)
            den_c = jnp.zeros((8, 2 * half), F32)
            den_r = jnp.zeros((8, half), F32)
            for k in range(2):
                for pair in range(2):
                    first = k * 4 + 2 * pair
                    left = jnp.concatenate(
                        [jnp.where(at8 == first + i, s_r, 0.0) for i in range(2)], axis=1
                    ).astype(BF16)
                    part = d_v[k * 2 + pair]
                    den_c += jnp.dot(left, part, preferred_element_type=F32)
                    got = across(s_c, part)
                    for i in range(2):
                        den_r = jnp.where(
                            at8 == first + i, got[:, i * half : (i + 1) * half], den_r
                        )
            rowd[step, c] = den_r
            send(rowd, c, (rd_s, rd_r), col_list, col_peer)
            cold[step, r] = den_c
            send(cold, r, (cd_s, cd_r), row_list, row_peer)

        def folded(x):
            return jnp.concatenate([x[0:4, :half], x[0:4, half:]], axis=0)

        def first_denominators():
            def own(sq):
                rows = [
                    jnp.where(e == 0, sq[4 * k : 4 * k + 2], sq[4 * k + 2 : 4 * k + 4])
                    for k in range(2)
                ]
                return jnp.concatenate(rows + [jnp.zeros_like(sq[0:4])], axis=0).astype(BF16)

            s_r, s_c = own(squared(g_f[...])), own(squared(gc))
            at = rows_like((8, 2 * half))
            den_c = jnp.zeros((8, 2 * half), F32)
            den_r = jnp.zeros((8, 2 * half), F32)
            for i in range(4):
                part = d0_v[i]
                got = jnp.dot(s_r, part, preferred_element_type=F32)
                den_c = jnp.where(at == i, got, den_c)
                den_r = jnp.where(at == i, across(s_c, part), den_r)
            rowds[step, c] = folded(den_r)
            colds[step, r] = folded(den_c)
            made = to_all(rowds, c, (rd_s, rd_r), col_list, col_peer)
            return made + to_all(colds, r, (cd_s, cd_r), row_list, row_peer)

        def channel(ch, _):
            if step == 0:
                chunk(ch, pl.ds(2 * other, 2)).wait_recv()
            picks = [idx[d, ch] for d in range(4)]
            before = [prev[d, ch] for d in range(4)]
            for t in range(half // TILE):
                rows = slice(t * TILE, (t + 1) * TILE)
                below = slice(half + t * TILE, half + (t + 1) * TILE)
                re, im = residual_tile(a_v, m_v if short else m_w, v_v, ch, picks, rows)
                w = w_v[ch, rows, :]
                re = re.astype(BF16) * w
                im = im.astype(BF16) * w
                for d in range(4):
                    m_re = m_v[d, 0, ch, rows, :]
                    m_im = m_v[d, 1, ch, rows, :]
                    old_re = t_v[before[d], d, rows, :]
                    old_im = t_v[before[d], d, below, :]
                    t_v[ch, d, rows, :] = old_re + (re * m_re + im * m_im)
                    t_v[ch, d, below, :] = old_im + (re * m_im - im * m_re)
            return 0

        def all_parts(product):
            out = jnp.zeros((16, 2 * half), F32)
            for k in range(2):
                for d in range(4):
                    keep = (at16 == 8 * k + d) | (at16 == 8 * k + 4 + d)
                    out = jnp.where(keep, product(t_v[last[k, d], d]), out)
            return out

        outer_products(a_v, gr, gc)
        if short:
            first = first_denominators()

            @pl.when(jnp.logical_not(holder))
            def _():
                for cp in first:
                    cp.start()

        else:
            denominators()
        lax.fori_loop(0, chans, channel, 0)
        if short:

            @pl.when(holder)
            def _():
                pl.semaphore_wait(late, len(partners) - 2)
                for cp in first:
                    cp.start()

        x_row = gc.astype(BF16)
        x_col = jnp.concatenate([gr, turned(gr)], axis=1).astype(BF16)
        o_row = all_parts(lambda part: across(x_row, part))
        o_row = o_row[:, :half] - turned(o_row[:, half:])
        if short:
            rowns[step, c] = o_row.astype(BF16)
            send(rowns, c, (rn_s, rn_r), col_list, col_peer)
        else:
            rown[step, c] = o_row + error[0]
            send(rown, c, (rn_s, rn_r), col_list, col_peer)
        o_col = all_parts(lambda part: jnp.dot(x_col, part, preferred_element_type=F32))
        if short:
            colns[step, r] = o_col.astype(BF16)
            send(colns, r, (cn_s, cn_r), row_list, row_peer)
            for l in range(2):
                squares(other, l, False)
            lax.fori_loop(0, chans, widen_model, 0)
            dens[e] = jnp.concatenate(
                [
                    gathered(colds, (cd_s, cd_r), r, n_row, row_list, row_peer),
                    gathered(rowds, (rd_s, rd_r), c, n_col, col_list, col_peer),
                ],
                axis=0,
            )
            dens_sib = remote(dens.at[e], dens.at[e], ds_s, ds_r.at[e], sib)
            dens_sib.start()
            copies.append(dens_sib)
        else:
            coln[step, r] = o_col + error[1]
            send(coln, r, (cn_s, cn_r), row_list, row_peer)
            for cp in local[6:8]:
                cp.wait()
            remote(
                model.at[:, :, their_ch, mine, :], mf_v.at[pl.ds(2 * other, 2)],
                mod_s.at[chans], mod_r.at[chans], sib,
            ).wait_recv()
            lax.fori_loop(0, fin, widen_rest, 0)

        def refresh(total, den):
            den = den + 1.0
            den = jnp.concatenate([den[0:4], den[0:4], den[4:8], den[4:8]], axis=0)
            return 0.5 * total / den

        total = gathered(colns if short else coln, (cn_s, cn_r), r, n_row, row_list, row_peer)
        if short:
            remote(dens.at[other], dens.at[other], ds_s, ds_r.at[other], sib).wait_recv()
            cores = []
            for i in range(2):
                part = dens[i]
                cores.append((
                    jnp.concatenate([part[0:4], part[4:8]], axis=1),
                    jnp.where(e == 0, part[8:12], part[12:16]),
                ))
            den_c, den_r = (
                jnp.concatenate([x[0:2], y[0:2], x[2:4], y[2:4]], axis=0)
                for x, y in zip(*cores)
            )
            total_den = jnp.zeros((8, 2 * half), F32)
        else:
            total_den = gathered(cold, (cd_s, cd_r), r, n_row, row_list, row_peer)
        colt[step, e] = jnp.concatenate([total, total_den], axis=0)
        both = remote(
            colt.at[step, e], colt.at[step, e], ct_s.at[step], ct_r.at[step, e], sib
        )
        both.start()
        copies.append(both)
        total = gathered(rowns if short else rown, (rn_s, rn_r), c, n_col, col_list, col_peer)
        if not short:
            den_r = gathered(rowd, (rd_s, rd_r), c, n_col, col_list, col_peer)
        change_r = refresh(total, den_r)
        g_r[...] = gr + change_r
        if step == ITERS - 1:
            g_r2[e] = g_r[...]
            rows_sib = remote(g_r2.at[e], g_r2.at[e], fin_s, fin_r.at[e], sib)
            rows_sib.start()
            copies.append(rows_sib)
        remote(
            colt.at[step, other], colt.at[step, other], ct_s.at[step], ct_r.at[step, other], sib
        ).wait_recv()
        total = colt[step, 0] + colt[step, 1]
        change_c = refresh(total[0:16], den_c if short else total[16:24])
        g_c[...] = gc + change_c
        if short:
            lost_r = o_row - rowns[step, c].astype(F32)
            lost_c = o_col - colns[step, r].astype(F32)
            error = (0.5 * lost_r, 0.5 * lost_c)
        return copies, error

    copies, error = [], None
    for step in range(ITERS):
        started, error = sweep(step, error)
        copies += started

    remote(g_r2.at[other], g_r2.at[other], fin_s, fin_r.at[other], sib).wait_recv()

    for cp in model_a + [model_b, gains_sib]:
        cp.wait_send()

    @pl.when(near)
    def _():
        for cp in gains_to(near_to):
            cp.wait_send()

    @pl.when(cross)
    def _():
        for cp in gains_to(cross_to):
            cp.wait_send()

    for cp in copies:
        cp.wait_send()


def finish_kernel(m_w, mf_w, v_w, g_r2, g_c, idx, gains_out, res_out, a_v, b_v, out_v, g_v, sem, g_sem):
    e = lax.axis_index("dir")
    half = m_w.shape[3]
    fin = mf_w.shape[2]
    g = g_c[...]
    for x in range(2):
        for l in range(2):
            for k in range(2):
                at = k * 8 + x * 4 + l
                g_v[x, l, k : k + 1, :] = jnp.where(e == 0, g[at : at + 1], g[at + 2 : at + 3])
    gains_copy = pltpu.make_async_copy(g_v, gains_out, g_sem)
    gains_copy.start()
    sides = (
        (m_w, v_w.at[0], e * fin, e),
        (mf_w, v_w.at[1], 0, 1 - e),
    )

    def moved(which, ch):
        side = sides[which][3]
        where = pl.ds(pl.multiple_of(side * half, half), half)
        return pltpu.make_async_copy(
            out_v.at[which, :, ch], res_out.at[:, ch, where, :], sem.at[which, ch]
        )

    products = (a_v, b_v)
    for which in range(2):
        outer_products(products[which], g_r2[sides[which][3]], g)
    for which, (mod, vi, base, side) in enumerate(sides):

        for ch in range(fin):
            picks = [idx[d, e * fin + ch] for d in range(4)]
            for t in range(half // TILE):
                rows = slice(t * TILE, (t + 1) * TILE)
                re, im = residual_tile(products[which], mod, vi, base + ch, picks, rows, ch)
                out_v[which, 0, ch, rows, :] = re
                out_v[which, 1, ch, rows, :] = im
            moved(which, ch).start()
    gains_copy.wait()
    for which in range(2):
        for ch in range(fin):
            moved(which, ch).wait()


def body(n_row, n_col, vis, model, gains, channel_interval_index, antenna_usable_mask):
    dirs, _, chans, rows, cols = model.shape
    half = rows // 2
    fin = chans // 2
    n_dir = 2 * dirs
    hbm = pl.BlockSpec(memory_space=pltpu.HBM)
    vmem = pl.BlockSpec(memory_space=pltpu.VMEM)
    smem = pl.BlockSpec(memory_space=pltpu.SMEM)
    dma = pltpu.SemaphoreType.DMA
    held = (
        pltpu.VMEM((n_dir, 2, chans, half, cols), F32),
        pltpu.VMEM((n_dir, 2, fin, half, cols), F32),
        pltpu.VMEM((2, 2, fin, half, cols), F32),
        pltpu.VMEM((2, 16, half), F32),
        pltpu.VMEM((16, cols), F32),
        pltpu.SMEM((n_dir, chans), jnp.int32),
    )
    spaces = (vmem,) * 5 + (smem,)
    args = [
        pltpu.with_memory_space_constraint(x, pltpu.HBM)
        for x in (vis, model, gains, antenna_usable_mask, channel_interval_index)
    ]
    state = pl.pallas_call(
        functools.partial(kernel, n_row, n_col),
        out_shape=held,
        in_specs=[hbm] * 5,
        out_specs=spaces,
        scratch_shapes=[
            pltpu.VMEM((n_dir, 2, chans, half, cols), BF16),
            pltpu.VMEM((2, chans, half, cols), BF16),
            pltpu.VMEM((n_dir, 2, fin, half, cols), BF16),
            pltpu.VMEM((2, fin, half, cols), BF16),
            pltpu.VMEM((2, 2, chans, half, cols), BF16),
            pltpu.VMEM((chans, half, cols), BF16),
            pltpu.VMEM((chans, half, cols), BF16),
            pltpu.VMEM((4, 2 * half, cols), BF16),
            pltpu.VMEM((4, 2 * half, cols), BF16),
            pltpu.VMEM((8, half, 2 * cols), F32),
            pltpu.VMEM((chans + 1, n_dir, 2 * half, cols), BF16),
            pltpu.VMEM((chans, half), jnp.int32),
            pltpu.VMEM((chans, half), jnp.int32),
            pltpu.VMEM((chans, cols), jnp.int32),
            pltpu.SMEM((n_dir, chans), jnp.int32),
            pltpu.SMEM((2, n_dir), jnp.int32),
            pltpu.VMEM((2,) + gains.shape, F32),
            pltpu.VMEM((2,) + gains.shape, F32),
            pltpu.VMEM((16, half), F32),
            pltpu.VMEM((ITERS, n_row, 16, cols), F32),
            pltpu.VMEM((ITERS, n_row, 8, cols), F32),
            pltpu.VMEM((ITERS, n_col, 16, half), F32),
            pltpu.VMEM((ITERS, n_col, 8, half), F32),
            pltpu.VMEM((1, n_row, 16, cols), BF16),
            pltpu.VMEM((1, n_row, 8, half), F32),
            pltpu.VMEM((1, n_col, 16, half), BF16),
            pltpu.VMEM((1, n_col, 8, half), F32),
            pltpu.VMEM((2, 16, half), F32),
            pltpu.VMEM((16, cols), F32),
            pltpu.VMEM((ITERS, 2, 24, cols), F32),
            pltpu.SemaphoreType.REGULAR,
            dma((10,)),
            dma((chans + 1,)),
            dma((chans + 1,)),
            dma,
            dma,
            dma((n_col,)),
            dma((2,)),
            dma((ITERS, n_row)),
            dma((ITERS, n_row)),
            dma((ITERS, n_row)),
            dma((ITERS, n_row)),
            dma((ITERS, n_col)),
            dma((ITERS, n_col)),
            dma((ITERS, n_col)),
            dma((ITERS, n_col)),
            dma((ITERS,)),
            dma((ITERS, 2)),
            dma,
            dma((2,)),
            dma,
            dma((2,)),
        ],
        compiler_params=pltpu.CompilerParams(
            collective_id=0, has_side_effects=True, vmem_limit_bytes=32 * 2**20
        ),
    )(*args)
    return pl.pallas_call(
        finish_kernel,
        out_shape=(
            pltpu.HBM(gains.shape, F32),
            pltpu.HBM((2, fin, rows, cols), F32),
        ),
        in_specs=spaces,
        out_specs=(hbm, hbm),
        scratch_shapes=[
            pltpu.VMEM((8, half, 2 * cols), F32),
            pltpu.VMEM((8, half, 2 * cols), F32),
            pltpu.VMEM((2, 2, fin, half, cols), F32),
            pltpu.VMEM(gains.shape, F32),
            dma((2, fin)),
            dma,
        ],
        compiler_params=pltpu.CompilerParams(vmem_limit_bytes=16 * 2**20),
    )(*state)


def solution(mesh):
    placed = (
        P(None, None, "row", "col"),
        P("dir", None, None, "row", "col"),
        P(None, "dir", None, "col"),
        P(),
        P(),
    )
    return jax.shard_map(
        functools.partial(body, mesh.shape["row"], mesh.shape["col"]),
        mesh=mesh,
        in_specs=placed,
        out_specs=(P(None, "dir", None, "col"), P(None, "dir", "row", "col")),
        check_vma=False,
    )
```
